128 devices in a mesh: chan: 16 (over y_lo, z, core), feed: 8 (over x, y_hi).
Axes of the slice: x: 4, y: 4 (y_hi: 2, y_lo: 2; y = y_hi * 2 + y_lo), z: 4, core: 2. Of those that a mesh axis runs over, the one named last changes fastest.
Arguments:
- raw_volts: bfloat16 [2048, 268288], P(('chan', 'feed')), may hold values from -6 to 6
- channel_gains: float32 [2, 64, 2048], P(None, None, ('chan', 'feed')), may hold values from -7 to 7
- feed_flags: int32 [2048], replicated, may hold values 0 or 1
- steer_index: int32 [512, 2048], P(None, 'feed'), may hold values from 0 to 255
Outputs:
- visibility: float32 [2, 64, 2048, 2048], P(None, 'chan', 'feed')
- beam_power: float32 [512, 64, 128], P('feed', 'chan')
The draws below stay inside these ranges and needn't reach their ends.
All inputs are finite; a program needn't handle non-finite values.
Results may differ from the reference program's by a relative error of at most 0.0053.
Values may be sent and summed in bfloat16 or wider, within the bound.
A program may use at most 128 MiB of HBM per device.

```python
import math
import jax
import jax.numpy as jnp
from jax import lax

CHANS = 1024
INPUTS = 2048
TAPS = 4
PHASES = 256
NT = 128
CH_BAND = 64
SAMPLES = 268288
BEAMS = 512


def draw_channel_gains(key, part):
    key = jax.random.fold_in(key, 11)
    first_key, second_key = jax.random.split(key)
    ramp = jnp.exp(0.5 * math.log(3.0) * jnp.arange(CH_BAND, dtype=jnp.float32) / max(CH_BAND - 1, 1))
    spread = jax.random.uniform(first_key, (CH_BAND, INPUTS), jnp.float32, math.log(0.5), math.log(2.0))
    magnitude = ramp[:, None] * jnp.exp(spread)
    phase_angle = jax.random.uniform(second_key, (CH_BAND, INPUTS), jnp.float32, -math.pi, math.pi)
    return jnp.stack([magnitude * jnp.cos(phase_angle), magnitude * jnp.sin(phase_angle)], axis=0)


def set_ends(entries, stream_key, least, top_value):
    extent = entries.shape
    index_at = [jax.random.randint(jax.random.fold_in(stream_key, axis), (), 0, extent[axis]) for axis in range(len(extent))]
    entries = entries.at[tuple(index_at)].set(least)
    longest = extent.index(max(extent))
    index_at[longest] = (index_at[longest] + 1) % extent[longest]
    return entries.at[tuple(index_at)].set(top_value)


def shard_levels(key, shape, pieces, least, high):
    def one(position, shards_of):
        steps = jax.random.uniform(jax.random.fold_in(jax.random.fold_in(key, 6), position), (shards_of,), jnp.float32, least / len(pieces), high / len(pieces))
        return jnp.repeat(jnp.exp(steps), shape[position] // shards_of).reshape((-1,) + (1,) * (len(shape) - position - 1))

    factor_of = one(*pieces[0])
    for cut in pieces[1:]:
        factor_of = factor_of * one(*cut)
    return factor_of


def noise(key, dims, scale, most, shards=(), kind=jnp.bfloat16):
    drawn = scale * jax.random.normal(key, dims, jnp.float32)
    if shards:
        drawn = drawn * shard_levels(key, dims, shards, -0.22, 0.18)
    return jnp.clip(drawn, -most, most).astype(kind)


def setup_inputs(seed: int = 0) -> dict:
    arg_keys = jax.random.split(jax.random.key(seed), 5)
    raw_volts = noise(arg_keys[0], (INPUTS, SAMPLES), 1.0, 6.0, ((0, 128),))
    channel_gains = draw_channel_gains(jax.random.fold_in(arg_keys[4], 71), 0)
    feed_flags = set_ends((jax.random.randint(arg_keys[2], (INPUTS,), 0, 8) < 7).astype(jnp.int32), jax.random.fold_in(arg_keys[2], 1), 0, 1)
    steer_index = set_ends(jax.random.randint(arg_keys[3], (BEAMS, INPUTS), 0, PHASES), jax.random.fold_in(arg_keys[3], 1), 0, PHASES - 1).astype(jnp.int32)
    return {"raw_volts": raw_volts, "channel_gains": channel_gains, "feed_flags": feed_flags, "steer_index": steer_index}


EPSILON = 1e-06

def filter_table(band_count):
    block_len = 2 * CHANS
    full_len = TAPS * block_len
    band_first = CHANS // 2 - band_count // 2
    sample_pos = jnp.arange(full_len, dtype=jnp.float32)
    centred = (sample_pos + 0.5) / full_len - 0.5
    window = jnp.sinc(TAPS * centred) * (0.5 - 0.5 * jnp.cos(2.0 * jnp.pi * (sample_pos + 0.5) / full_len))
    window = window / jnp.sqrt(jnp.sum(window * window))
    within = jnp.arange(block_len, dtype=jnp.int32)
    channel = band_first + jnp.arange(band_count, dtype=jnp.int32)
    turn_count = within[:, None] * channel[None, :] % block_len
    phase_angle = 2.0 * jnp.pi / block_len * turn_count.astype(jnp.float32)
    weights = window.reshape(TAPS, block_len)[:, :, None]
    combined = jnp.concatenate([weights * jnp.cos(phase_angle)[None], -(weights * jnp.sin(phase_angle)[None])], axis=2)
    return combined.astype(jnp.bfloat16)

def channelize(volt_rows, table):
    row_count = volt_rows.shape[0]
    block_len = 2 * CHANS
    spectra = volt_rows.shape[1] // block_len - TAPS + 1
    blocks = volt_rows.astype(jnp.float32).reshape(row_count, spectra + TAPS - 1, block_len)
    wide_table = table.astype(jnp.float32)
    summed = jnp.zeros((row_count * spectra, table.shape[2]), jnp.float32)
    for tap_index in range(TAPS):
        frames = blocks[:, tap_index:tap_index + spectra].reshape(row_count * spectra, block_len)
        summed = summed + jnp.dot(frames, wide_table[tap_index], preferred_element_type=jnp.float32)
    return summed.reshape(row_count, spectra, table.shape[2])

def apply_gains(raw_spectra, gain_rows):
    band_count = raw_spectra.shape[2] // 2
    real_part = raw_spectra[:, :, :band_count]
    imag_part = raw_spectra[:, :, band_count:]
    gain_re = gain_rows[0].T[:, None, :]
    gain_im = gain_rows[1].T[:, None, :]
    real_spec = (gain_re * real_part - gain_im * imag_part).astype(jnp.bfloat16)
    imag_spec = (gain_re * imag_part + gain_im * real_part).astype(jnp.bfloat16)
    return (real_spec, imag_spec)

def reference(raw_volts, channel_gains, feed_flags, steer_index):
    table = filter_table(CH_BAND)
    group_rows = 64
    volt_groups = raw_volts.reshape(INPUTS // group_rows, group_rows, SAMPLES)
    gain_groups = channel_gains.reshape(2, CH_BAND, INPUTS // group_rows, group_rows).transpose(2, 0, 1, 3)

    def one_group(operands):
        raw_spectra = channelize(operands[0], table)
        return apply_gains(raw_spectra, operands[1])
    real_spec, imag_spec = lax.map(one_group, (volt_groups, gain_groups))
    real_spec = real_spec.reshape(INPUTS, NT, CH_BAND)
    imag_spec = imag_spec.reshape(INPUTS, NT, CH_BAND)
    wide_re = real_spec.astype(jnp.float32)
    wide_im = imag_spec.astype(jnp.float32)
    band_mean = lax.optimization_barrier(jnp.sum(wide_re * wide_re + wide_im * wide_im, axis=(1, 2))) / (CH_BAND * NT)
    inverse_rms = lax.rsqrt(band_mean + EPSILON)
    flag_values = feed_flags.astype(jnp.bfloat16)[:, None, None]
    masked_re = jnp.moveaxis(real_spec * flag_values, 2, 0)
    masked_im = jnp.moveaxis(imag_spec * flag_values, 2, 0)
    phase_angle = 2.0 * jnp.pi / PHASES * steer_index.astype(jnp.float32)
    cos_weight = jnp.cos(phase_angle).astype(jnp.bfloat16).astype(jnp.float32)
    sin_weight = jnp.sin(phase_angle).astype(jnp.bfloat16).astype(jnp.float32)
    pair_weight = inverse_rms[:, None] * inverse_rms[None, :] / NT

    def one_channel(operands):
        part_re = operands[0].astype(jnp.float32)
        part_im = operands[1].astype(jnp.float32)
        stacked = jnp.concatenate([part_re, part_im], axis=1)
        swapped = jnp.concatenate([part_im, -part_re], axis=1)
        real_vis = jnp.dot(stacked, stacked.T, preferred_element_type=jnp.float32) * pair_weight
        imag_vis = jnp.dot(swapped, stacked.T, preferred_element_type=jnp.float32) * pair_weight
        beam_re = jnp.dot(cos_weight, part_re, preferred_element_type=jnp.float32) - jnp.dot(sin_weight, part_im, preferred_element_type=jnp.float32)
        beam_im = jnp.dot(sin_weight, part_re, preferred_element_type=jnp.float32) + jnp.dot(cos_weight, part_im, preferred_element_type=jnp.float32)
        return (real_vis, imag_vis, (beam_re * beam_re + beam_im * beam_im) / INPUTS)
    real_all, imag_all, beam_all = lax.map(one_channel, (masked_re, masked_im))
    visibility = jnp.stack([real_all, imag_all], axis=0)
    beam_power = jnp.transpose(beam_all, (1, 0, 2))
    return (visibility, beam_power)
```

```python
import functools

import jax
import jax.numpy as jnp
import ml_dtypes
import numpy as np
from jax import lax
from jax.experimental import pallas as pl
from jax.experimental.pallas import tpu as pltpu
from jax.sharding import PartitionSpec as P

CHANS = 1024
INPUTS = 2048
TAPS = 4
PHASES = 256
NT = 128
BAND = 64
BEAMS = 512
BLOCK = 2 * CHANS
EPSILON = 1e-06

CHAN_DEVS = 16
FEED_DEVS = 8
OWN = 16
PER_CHAN = BAND // CHAN_DEVS
UNIT = PER_CHAN * OWN
HALF_T = NT // 2
SLABS = NT + TAPS - 1
SUBS = 2
SUB = CHAN_DEVS // SUBS
OWN_BEAMS = BEAMS // FEED_DEVS
FEED_INPUTS = INPUTS // FEED_DEVS
KINDS = 7
FIRST_SLABS = 68
MESH = pl.DeviceIdType.MESH


def filter_table():
    full_len = TAPS * BLOCK
    pos = np.arange(full_len, dtype=np.float64)
    centred = (pos + 0.5) / full_len - 0.5
    window = np.sinc(TAPS * centred) * (0.5 - 0.5 * np.cos(2.0 * np.pi * (pos + 0.5) / full_len))
    window = window / np.sqrt(np.sum(window * window))
    channel = CHANS // 2 - BAND // 2 + np.arange(BAND)
    turn = (np.arange(BLOCK)[:, None] * channel[None, :]) % BLOCK
    angle = 2.0 * np.pi / BLOCK * turn
    weights = window.reshape(TAPS, BLOCK)[:, :, None]
    table = np.concatenate([weights * np.cos(angle), -(weights * np.sin(angle))], axis=2)
    return np.transpose(table, (1, 0, 2)).reshape(BLOCK, TAPS * 2 * BAND).astype(ml_dtypes.bfloat16)


def turn_kernel(
    raw, table, gains, steer, flags, spectra, powers, weights,
    volts, tab, conv, summed, turned, outbox, gain_sq, power_acc, power_row,
    steer_out, steer_in, weight_buf,
    load_sem, tab_sem, own_sem, a_send, a_recv, b_send, b_recv,
    s_send, s_recv, p_send, p_recv, q_send, q_recv, out_sem,
):
    chan = lax.axis_index("chan")
    feed = lax.axis_index("feed")
    x = feed // 2
    row = feed % 2

    def feed_at(dx, across):
        r = 1 - row if across else row
        return lax.rem(x + dx + 4, 4) * 2 + r

    right = (chan, feed_at(1, False))
    left = (chan, feed_at(-1, False))
    over = (chan, feed_at(0, True))

    barrier = pltpu.get_barrier_semaphore()
    for d in range(1, CHAN_DEVS):
        pl.semaphore_signal(
            barrier, inc=1, device_id=(lax.rem(chan + d, CHAN_DEVS), feed), device_id_type=MESH
        )
    for d in range(1, FEED_DEVS):
        pl.semaphore_signal(
            barrier, inc=1, device_id=(chan, lax.rem(feed + d, FEED_DEVS)), device_id_type=MESH
        )

    tab_copy = pltpu.make_async_copy(table, tab, tab_sem)
    tab_copy.start()
    groups = [(0, 34), (34, 34), (68, 32), (100, 31)]
    for g, (first, count) in enumerate(groups):

        @pl.loop(0, count)
        def _(n):
            s = first + n
            pltpu.make_async_copy(
                raw.at[:, pl.ds(pl.multiple_of(s * BLOCK, BLOCK), BLOCK)],
                volts.at[pl.ds(pl.multiple_of(s * OWN, OWN), OWN), :],
                load_sem.at[g],
            ).start()

    steer_out[...] = steer[...].astype(jnp.float32).astype(jnp.bfloat16)

    gain_sq[...] = jnp.zeros_like(gain_sq)
    gain_sq[0:BAND, 0:OWN] = gains[0]
    gain_sq[BAND : 2 * BAND, 0:OWN] = gains[1]
    gain_rows = gain_sq[...].T[0:OWN]
    lane8 = lax.broadcasted_iota(jnp.int32, (8, 128), 1)
    low8 = lane8 < BAND
    g_lo, g_hi = gain_rows[0:8], gain_rows[8:16]
    pair_re = jnp.where(low8, g_lo, pltpu.roll(g_hi, BAND, 1))
    pair_im = jnp.where(low8, pltpu.roll(g_lo, BAND, 1), g_hi)

    pl.semaphore_wait(barrier, CHAN_DEVS + FEED_DEVS - 2)

    steer_copies = []
    for d in range(1, FEED_DEVS):
        other = lax.rem(feed + d, FEED_DEVS)
        steer_copies.append(
            pltpu.make_async_remote_copy(
                src_ref=steer_out.at[pl.ds(pl.multiple_of(other * OWN_BEAMS, OWN_BEAMS), OWN_BEAMS), :],
                dst_ref=steer_in.at[feed],
                send_sem=s_send.at[d],
                recv_sem=s_recv.at[d],
                device_id=(chan, other),
                device_id_type=MESH,
            )
        )
        steer_copies[-1].start()
    own_steer = pltpu.make_async_copy(
        steer_out.at[pl.ds(pl.multiple_of(feed * OWN_BEAMS, OWN_BEAMS), OWN_BEAMS), :],
        steer_in.at[feed],
        s_send.at[0],
    )
    own_steer.start()

    low = lax.broadcasted_iota(jnp.int32, (HALF_T, 128), 1) < BAND

    def loaded(g):
        first, count = groups[g]
        rows = volts.at[pl.ds(first * OWN, count * OWN), :]
        pltpu.make_async_copy(rows, rows, load_sem.at[g]).wait()

    def convolve(first, count):
        conv[pl.ds(first * OWN, count * OWN), :] = jnp.dot(
            volts[pl.ds(first * OWN, count * OWN), :], tab[...], preferred_element_type=jnp.float32
        )

    def turn(h):
        total = None
        for k in range(TAPS):
            part = conv[pl.ds((HALF_T * h + k) * OWN, HALF_T * OWN), 128 * k : 128 * (k + 1)]
            total = part if total is None else total + part
        summed[...] = total
        for i in range(8):
            a = summed[pl.ds(i, HALF_T, stride=OWN), :]
            b = summed[pl.ds(i + 8, HALF_T, stride=OWN), :]
            re = jnp.where(low, a, pltpu.roll(b, BAND, 1))
            im = jnp.where(low, pltpu.roll(a, BAND, 1), b)
            g_re = pair_re[i : i + 1]
            g_im = pair_im[i : i + 1]
            spec_re = (g_re * re - g_im * im).astype(jnp.bfloat16).astype(jnp.float32)
            spec_im = (g_re * im + g_im * re).astype(jnp.bfloat16).astype(jnp.float32)
            power = spec_re * spec_re + spec_im * spec_im
            power = jnp.sum(power.reshape(HALF_T // 8, 8, 128), axis=0)
            if h == 0:
                power_acc[i] = power
            else:
                power_acc[i] = power_acc[i] + power
            flipped = jnp.concatenate([spec_re, spec_im], axis=0).T
            turned[pl.ds(i, BAND, stride=OWN), :] = flipped[0:BAND]
            turned[pl.ds(i + 8, BAND, stride=OWN), :] = flipped[BAND : 2 * BAND]
        outbox[h] = turned[...].astype(jnp.bfloat16)

    a_copies = []

    def send_chan(h):
        mine = pltpu.make_async_copy(
            outbox.at[h, pl.ds(pl.multiple_of(chan * UNIT, UNIT), UNIT), :],
            spectra.at[h, chan, feed],
            own_sem.at[h],
        )
        mine.start()
        for d in range(1, CHAN_DEVS):
            other = lax.rem(chan + d, CHAN_DEVS)
            copy = pltpu.make_async_remote_copy(
                src_ref=outbox.at[h, pl.ds(pl.multiple_of(other * UNIT, UNIT), UNIT), :],
                dst_ref=spectra.at[h, chan, feed],
                send_sem=a_send.at[h, d],
                recv_sem=a_recv.at[h, chan // SUB],
                device_id=(other, feed),
                device_id_type=MESH,
            )
            copy.start()
            a_copies.append(copy)
        return mine

    def arrived(h, sub, count):
        rows = spectra.at[h, pl.ds(0, count), 0]
        pltpu.make_async_copy(rows, rows, a_recv.at[h, sub]).wait()

    sub_of = [chan // SUB, 1 - chan // SUB]

    def spread(h, n, kind, origin, target):
        block = spectra.at[h, pl.ds(pl.multiple_of(sub_of[n] * SUB, SUB), SUB), origin]
        return pltpu.make_async_remote_copy(
            src_ref=block,
            dst_ref=block,
            send_sem=b_send.at[h, kind, n],
            recv_sem=b_recv.at[h, kind, n],
            device_id=target,
            device_id_type=MESH,
        )

    plans = []
    for h in range(2):
        fore, back = (right, left) if h == 0 else (left, right)
        s = 1 if h == 0 else -1
        plans.append(
            [
                (feed, fore),
                (feed, back),
                (feed, over),
                (feed_at(-s, False), fore),
                (feed_at(s, False), over),
                (feed_at(0, True), fore),
                (feed_at(s, True), back),
            ]
        )
    made = {}

    def start(h, n, kind):
        origin, target = plans[h][kind]
        made[h, n, kind] = spread(h, n, kind, origin, target)
        made[h, n, kind].start()

    def landed(h, n, kind):
        made[h, n, kind].wait_recv()

    def step_one(h, n, mine):
        if n == 0:
            mine.wait()
            arrived(h, sub_of[0], SUB - 1)
        else:
            arrived(h, sub_of[1], SUB)
        for kind in (2, 0, 1):
            start(h, n, kind)

    loaded(0)
    tab_copy.wait()
    convolve(0, 34)
    loaded(1)
    convolve(34, 34)
    turn(0)
    mine0 = send_chan(0)
    loaded(2)
    convolve(67, 33)
    loaded(3)
    convolve(100, 31)
    step_one(0, 0, mine0)
    turn(1)
    mine1 = send_chan(1)
    step_one(0, 1, mine0)

    sums = jnp.sum(power_acc[...], axis=1)
    first = jnp.sum(jnp.where(low8, sums, 0.0), axis=1, keepdims=True)
    second = jnp.sum(jnp.where(low8, 0.0, sums), axis=1, keepdims=True)
    column = jnp.concatenate([first, second], axis=0)
    lane16 = lax.broadcasted_iota(jnp.int32, (OWN, 128), 1)
    sub16 = lax.broadcasted_iota(jnp.int32, (OWN, 128), 0)
    power_row[...] = jnp.sum(
        jnp.where(lax.rem(lane16, OWN) == sub16, column, 0.0), axis=0, keepdims=True
    )
    p_own = pltpu.make_async_copy(power_row, powers.at[feed, chan], own_sem.at[2])
    p_own.start()
    p_copies = []
    for d in range(1, CHAN_DEVS):
        copy = pltpu.make_async_remote_copy(
            src_ref=power_row,
            dst_ref=powers.at[feed, chan],
            send_sem=p_send.at[d],
            recv_sem=p_recv.at[d],
            device_id=(lax.rem(chan + d, CHAN_DEVS), feed),
            device_id_type=MESH,
        )
        copy.start()
        p_copies.append(copy)

    step_one(1, 0, mine1)
    step_one(1, 1, mine1)

    for copy in steer_copies:
        copy.wait()
    own_steer.wait()
    for g in range(FEED_DEVS):
        cols = pl.ds(g * FEED_INPUTS, FEED_INPUTS)
        index = steer_in[g].astype(jnp.float32)
        quarter = jnp.floor((index + 32.0) * (1.0 / 64.0))
        angle = (index - 64.0 * quarter) * (2.0 * np.pi / PHASES)
        sq = angle * angle
        cos = 1.0 + sq * (-1.0 / 2 + sq * (1.0 / 24 + sq * (-1.0 / 720 + sq * (1.0 / 40320))))
        sin = angle * (
            1.0 + sq * (-1.0 / 6 + sq * (1.0 / 120 + sq * (-1.0 / 5040 + sq * (1.0 / 362880))))
        )
        swap = (quarter == 1.0) | (quarter == 3.0)
        cos_neg = (quarter == 1.0) | (quarter == 2.0)
        sin_neg = (quarter == 2.0) | (quarter == 3.0)
        cos_mag = jnp.where(swap, sin, cos)
        sin_mag = jnp.where(swap, cos, sin)
        good = flags[:, cols].astype(jnp.float32)
        weight_buf[0:OWN_BEAMS, cols] = (jnp.where(cos_neg, -cos_mag, cos_mag) * good).astype(
            jnp.bfloat16
        )
        weight_buf[OWN_BEAMS : 2 * OWN_BEAMS, cols] = (
            jnp.where(sin_neg, -sin_mag, sin_mag) * good
        ).astype(jnp.bfloat16)
    weight_copy = pltpu.make_async_copy(weight_buf, weights, out_sem)
    weight_copy.start()

    for h in range(2):
        fore_in, back_in = 0, 1
        for n in range(SUBS):
            landed(h, n, back_in)
            start(h, n, 4)
            landed(h, n, fore_in)
            start(h, n, 3)
            landed(h, n, 2)
            start(h, n, 5)

    p_own.wait()
    for copy in p_copies:
        copy.wait()
    q_copies = []
    for d in range(1, FEED_DEVS):
        copy = pltpu.make_async_remote_copy(
            src_ref=powers.at[feed],
            dst_ref=powers.at[feed],
            send_sem=q_send.at[d],
            recv_sem=q_recv.at[d],
            device_id=(chan, lax.rem(feed + d, FEED_DEVS)),
            device_id_type=MESH,
        )
        copy.start()
        q_copies.append(copy)

    for h in range(2):
        for n in range(SUBS):
            landed(h, n, 4)
            start(h, n, 6)

    for copy in a_copies:
        copy.wait_send()
    for copy in q_copies:
        copy.wait()
    weight_copy.wait()
    for h in range(2):
        for n in range(SUBS):
            for kind in (3, 5, 6):
                landed(h, n, kind)
    for h in range(2):
        for n in range(SUBS):
            for kind in range(KINDS):
                made[h, n, kind].wait_send()


def correlate_kernel(spectra, powers, flags, weights, vis, beam, col_scale, row_scale):
    feed = lax.axis_index("feed")
    c = pl.program_id(0)
    j = pl.program_id(1)

    @pl.when((c == 0) & (j == 0))
    def _():
        lane = lax.broadcasted_iota(jnp.int32, (CHAN_DEVS, 128), 1)
        power = jnp.zeros((CHAN_DEVS, 128), jnp.float32)
        for f in range(FEED_DEVS):
            power = jnp.where(lane // OWN == f, powers[f].reshape(CHAN_DEVS, 128), power)
        scale = lax.rsqrt(power / (BAND * NT) + EPSILON)
        col_scale[...] = scale * flags[...].astype(jnp.float32)
        for n in range(2):
            one = col_scale[pl.ds(2 * feed + n, 1), :] * (1.0 / NT)
            row_scale[128 * n : 128 * (n + 1), :] = jnp.broadcast_to(one, (128, 128)).T

    def parts(first, count):
        return jnp.concatenate(
            [
                spectra[h, pl.ds(first, count)].reshape(count * 128, 128)
                for h in range(2)
            ],
            axis=1,
        )

    def swapped(h):
        own = spectra[h, pl.ds(2 * feed, 2)].reshape(256, 128).astype(jnp.float32)
        lane = lax.broadcasted_iota(jnp.int32, (256, 128), 1)
        turned = pltpu.roll(own, HALF_T, 1)
        return jnp.where(lane < HALF_T, turned, -turned).astype(jnp.bfloat16)

    own = parts(2 * feed, 2)
    left = jnp.concatenate([own, jnp.concatenate([swapped(0), swapped(1)], axis=1)], axis=0)
    rows = row_scale[...]
    contract = (((1,), (1,)), ((), ()))
    tiles = vis.shape[3] // 256
    for n in range(tiles):
        right = parts(j * 2 * tiles + 2 * n, 2)
        both = lax.dot_general(left, right, contract, preferred_element_type=jnp.float32)
        for m in range(2):
            scale = rows * col_scale[pl.ds(j * 2 * tiles + 2 * n + m, 1), :]
            out = pl.ds((2 * n + m) * 128, 128)
            vis[0, 0, :, out] = both[0:256, 128 * m : 128 * (m + 1)] * scale
            vis[1, 0, :, out] = both[256:512, 128 * m : 128 * (m + 1)] * scale

    @pl.when(j == 0)
    def _():
        lane = lax.broadcasted_iota(jnp.int32, (OWN_BEAMS, 128), 1)
        halves = []
        for h in range(2):
            sums = jnp.dot(
                weights[...],
                spectra[h].reshape(INPUTS, 128),
                preferred_element_type=jnp.float32,
            )
            cos_part = sums[0:OWN_BEAMS]
            sin_part = pltpu.roll(sums[OWN_BEAMS : 2 * OWN_BEAMS], HALF_T, 1)
            field = cos_part + jnp.where(lane < HALF_T, -sin_part, sin_part)
            square = field * field
            halves.append(square + pltpu.roll(square, HALF_T, 1))
        power = jnp.where(lane < HALF_T, halves[0], halves[1]) * (1.0 / INPUTS)
        for n in range(PER_CHAN):

            @pl.when(c == n)
            def _():
                beam[:, n, :] = power


def on_device(table, raw_volts, channel_gains, feed_flags, steer_index):
    vmem = pl.BlockSpec(memory_space=pltpu.VMEM)
    hbm = pl.BlockSpec(memory_space=pl.ANY)
    bf16, f32 = jnp.bfloat16, jnp.float32
    dma = pltpu.SemaphoreType.DMA
    spectra, powers, weights = pl.pallas_call(
        turn_kernel,
        name="channelize_turn",
        out_shape=(
            jax.ShapeDtypeStruct((2, CHAN_DEVS, FEED_DEVS, UNIT, 128), bf16),
            jax.ShapeDtypeStruct((FEED_DEVS, CHAN_DEVS, 1, 128), f32),
            jax.ShapeDtypeStruct((2 * OWN_BEAMS, INPUTS), bf16),
        ),
        in_specs=[hbm, hbm, vmem, vmem, vmem],
        out_specs=(hbm, hbm, hbm),
        scratch_shapes=[
            pltpu.VMEM((SLABS * OWN, BLOCK), bf16),
            pltpu.VMEM((BLOCK, TAPS * 128), bf16),
            pltpu.VMEM((SLABS * OWN, TAPS * 128), f32),
            pltpu.VMEM((HALF_T * OWN, 128), f32),
            pltpu.VMEM((BAND * OWN, 128), f32),
            pltpu.VMEM((2, BAND * OWN, 128), bf16),
            pltpu.VMEM((128, 128), f32),
            pltpu.VMEM((8, 8, 128), f32),
            pltpu.VMEM((1, 128), f32),
            pltpu.VMEM((BEAMS, FEED_INPUTS), bf16),
            pltpu.VMEM((FEED_DEVS, OWN_BEAMS, FEED_INPUTS), bf16),
            pltpu.VMEM((2 * OWN_BEAMS, INPUTS), bf16),
            dma((4,)),
            dma,
            dma((3,)),
            dma((2, CHAN_DEVS)),
            dma((2, SUBS)),
            dma((2, KINDS, SUBS)),
            dma((2, KINDS, SUBS)),
            dma((FEED_DEVS,)),
            dma((FEED_DEVS,)),
            dma((CHAN_DEVS,)),
            dma((CHAN_DEVS,)),
            dma((FEED_DEVS,)),
            dma((FEED_DEVS,)),
            dma,
        ],
        compiler_params=pltpu.CompilerParams(
            collective_id=0, has_side_effects=True, vmem_limit_bytes=48 * 2**20
        ),
        cost_estimate=pl.CostEstimate(
            flops=2 * SLABS * OWN * BLOCK * 512, bytes_accessed=20_000_000, transcendentals=0
        ),
    )(raw_volts, table, channel_gains, steer_index, feed_flags.reshape(1, INPUTS))

    cols = 1024
    steps = INPUTS // cols
    visibility, beam_power = pl.pallas_call(
        correlate_kernel,
        name="correlate",
        grid=(PER_CHAN, steps),
        out_shape=(
            jax.ShapeDtypeStruct((2, PER_CHAN, FEED_INPUTS, INPUTS), f32),
            jax.ShapeDtypeStruct((OWN_BEAMS, PER_CHAN, NT), f32),
        ),
        in_specs=[
            pl.BlockSpec((2, CHAN_DEVS, FEED_DEVS, OWN, 128), lambda c, j: (0, 0, 0, c, 0)),
            pl.BlockSpec((FEED_DEVS, CHAN_DEVS, 1, 128), lambda c, j: (0, 0, 0, 0)),
            pl.BlockSpec((CHAN_DEVS, 128), lambda c, j: (0, 0)),
            pl.BlockSpec((2 * OWN_BEAMS, INPUTS), lambda c, j: (0, 0)),
        ],
        out_specs=(
            pl.BlockSpec((2, 1, FEED_INPUTS, cols), lambda c, j: (0, c, 0, j)),
            pl.BlockSpec((OWN_BEAMS, PER_CHAN, NT), lambda c, j: (0, 0, 0)),
        ),
        scratch_shapes=[pltpu.VMEM((CHAN_DEVS, 128), f32), pltpu.VMEM((256, 128), f32)],
        compiler_params=pltpu.CompilerParams(vmem_limit_bytes=48 * 2**20),
        cost_estimate=pl.CostEstimate(
            flops=2_700_000_000, bytes_accessed=22_000_000, transcendentals=0
        ),
    )(spectra, powers, feed_flags.reshape(CHAN_DEVS, 128), weights)
    return (visibility, beam_power)


def solution(mesh):
    table = filter_table()
    in_specs = (P(("chan", "feed"), None), P(None, None, ("chan", "feed")), P(), P(None, "feed"))
    out_specs = (P(None, "chan", "feed", None), P("feed", "chan", None))

    def body(raw_volts, channel_gains, feed_flags, steer_index):
        return on_device(
            jnp.asarray(table), raw_volts, channel_gains, feed_flags, steer_index
        )

    return jax.shard_map(
        body, mesh=mesh, in_specs=in_specs, out_specs=out_specs, check_vma=False
    )
```

```python
import functools

import jax
import jax.numpy as jnp
import ml_dtypes
import numpy as np
from jax import lax
from jax.experimental import pallas as pl
from jax.experimental.pallas import tpu as pltpu
from jax.sharding import PartitionSpec as P

CHANS = 1024
INPUTS = 2048
TAPS = 4
PHASES = 256
NT = 128
BAND = 64
BEAMS = 512
BLOCK = 2 * CHANS
EPSILON = 1e-06

CHAN_DEVS = 16
FEED_DEVS = 8
OWN = 16
PER_CHAN = BAND // CHAN_DEVS
UNIT = PER_CHAN * OWN
HALF_T = NT // 2
SLABS = NT + TAPS - 1
SUBS = 2
SUB = CHAN_DEVS // SUBS
OWN_BEAMS = BEAMS // FEED_DEVS
FEED_INPUTS = INPUTS // FEED_DEVS
KINDS = 6
OUT_PARTS = 4
IN_PARTS = 1
MESH = pl.DeviceIdType.MESH


def filter_table():
    full_len = TAPS * BLOCK
    pos = np.arange(full_len, dtype=np.float64)
    centred = (pos + 0.5) / full_len - 0.5
    window = np.sinc(TAPS * centred) * (0.5 - 0.5 * np.cos(2.0 * np.pi * (pos + 0.5) / full_len))
    window = window / np.sqrt(np.sum(window * window))
    channel = CHANS // 2 - BAND // 2 + np.arange(BAND)
    turn = (np.arange(BLOCK)[:, None] * channel[None, :]) % BLOCK
    angle = 2.0 * np.pi / BLOCK * turn
    weights = window.reshape(TAPS, BLOCK)[:, :, None]
    table = np.concatenate([weights * np.cos(angle), -(weights * np.sin(angle))], axis=2)
    return np.transpose(table, (1, 0, 2)).reshape(BLOCK, TAPS * 2 * BAND).astype(ml_dtypes.bfloat16)


def turn_kernel(
    raw, table, gains, steer, flags, spectra, powers, weights,
    volts, tab, conv, summed, turned, outbox, gain_buf, steer_buf, flag_buf, power_acc, power_row,
    steer_out, steer_in, weight_buf,
    load_sem, tab_sem, small_sem, own_sem, a_send, a_recv, b_send, b_recv,
    s_send, s_recv, p_send, p_recv, q_send, q_recv, out_sem,
):
    chan = lax.axis_index("chan")
    feed = lax.axis_index("feed")
    x = feed // 2
    row = feed % 2

    def feed_at(dx, across):
        r = 1 - row if across else row
        return lax.rem(x + dx + 4, 4) * 2 + r

    right = (chan, feed_at(1, False))
    left = (chan, feed_at(-1, False))
    over = (chan, feed_at(0, True))

    barrier = pltpu.get_barrier_semaphore()
    plane = [
        ((half, d), across)
        for half in range(SUBS)
        for across in range(2)
        for d in range(SUB)
        if (half, d, across) != (0, 0, 0)
    ]

    def plane_peer(half, d):
        first = (chan // SUB + half) % SUBS * SUB
        return first + lax.rem(chan + d, SUB)

    distant = [(dx, across) for dx in (1, 3, 2) for across in (False, True)]
    for (half, d), across in plane:
        pl.semaphore_signal(
            barrier,
            inc=1,
            device_id=(plane_peer(half, d), feed_at(0, bool(across))),
            device_id_type=MESH,
        )
    for dx, across in distant:
        pl.semaphore_signal(
            barrier, inc=1, device_id=(chan, feed_at(dx, across)), device_id_type=MESH
        )

    tab_copy = pltpu.make_async_copy(table, tab, tab_sem)
    tab_copy.start()
    gain_copy = pltpu.make_async_copy(gains, gain_buf, small_sem.at[0])
    gain_copy.start()
    steer_copy = pltpu.make_async_copy(steer, steer_buf, small_sem.at[1])
    steer_copy.start()
    flag_copy = pltpu.make_async_copy(flags, flag_buf, small_sem.at[2])
    flag_copy.start()
    groups = [(0, 34), (34, 34), (68, 32), (100, 31)]
    for g, (first, count) in enumerate(groups):

        @pl.loop(0, count)
        def _(n):
            s = first + n
            pltpu.make_async_copy(
                raw.at[:, pl.ds(pl.multiple_of(s * BLOCK, BLOCK), BLOCK)],
                volts.at[pl.ds(pl.multiple_of(s * OWN, OWN), OWN), :],
                load_sem.at[g],
            ).start()

    steer_copy.wait()
    steer_out[...] = steer_buf[...].astype(jnp.float32).astype(jnp.bfloat16)

    gain_copy.wait()
    pair_re = jnp.concatenate([gain_buf[0, 0:8], gain_buf[0, 8:16]], axis=1)
    pair_im = jnp.concatenate([gain_buf[1, 0:8], gain_buf[1, 8:16]], axis=1)
    lane8 = lax.broadcasted_iota(jnp.int32, (8, 128), 1)
    low8 = lane8 < BAND

    pl.semaphore_wait(barrier, len(plane) + len(distant))

    steer_copies = []
    for d in range(1, FEED_DEVS):
        other = lax.rem(feed + d, FEED_DEVS)
        steer_copies.append(
            pltpu.make_async_remote_copy(
                src_ref=steer_out.at[pl.ds(pl.multiple_of(other * OWN_BEAMS, OWN_BEAMS), OWN_BEAMS), :],
                dst_ref=steer_in.at[feed],
                send_sem=s_send.at[d],
                recv_sem=s_recv.at[d],
                device_id=(chan, other),
                device_id_type=MESH,
            )
        )
        steer_copies[-1].start()
    own_steer = pltpu.make_async_copy(
        steer_out.at[pl.ds(pl.multiple_of(feed * OWN_BEAMS, OWN_BEAMS), OWN_BEAMS), :],
        steer_in.at[feed],
        s_send.at[0],
    )
    own_steer.start()

    low = lax.broadcasted_iota(jnp.int32, (HALF_T, 128), 1) < BAND

    def loaded(g):
        first, count = groups[g]
        rows = volts.at[pl.ds(first * OWN, count * OWN), :]
        pltpu.make_async_copy(rows, rows, load_sem.at[g]).wait()

    def convolve(first, count):
        conv[pl.ds(first * OWN, count * OWN), :] = jnp.dot(
            volts[pl.ds(first * OWN, count * OWN), :], tab[...], preferred_element_type=jnp.float32
        )

    def turn(h):
        total = None
        for k in range(TAPS):
            part = conv[pl.ds((HALF_T * h + k) * OWN, HALF_T * OWN), 128 * k : 128 * (k + 1)]
            total = part if total is None else total + part
        summed[...] = total
        for i in range(8):
            a = summed[pl.ds(i, HALF_T, stride=OWN), :]
            b = summed[pl.ds(i + 8, HALF_T, stride=OWN), :]
            re = jnp.where(low, a, pltpu.roll(b, BAND, 1))
            im = jnp.where(low, pltpu.roll(a, BAND, 1), b)
            g_re = pair_re[i : i + 1]
            g_im = pair_im[i : i + 1]
            spec_re = (g_re * re - g_im * im).astype(jnp.bfloat16).astype(jnp.float32)
            spec_im = (g_re * im + g_im * re).astype(jnp.bfloat16).astype(jnp.float32)
            power = spec_re * spec_re + spec_im * spec_im
            power = jnp.sum(power.reshape(HALF_T // 8, 8, 128), axis=0)
            if h == 0:
                power_acc[i] = power
            else:
                power_acc[i] = power_acc[i] + power
            flipped = jnp.concatenate([spec_re, spec_im], axis=0).T
            turned[pl.ds(i, BAND, stride=OWN), :] = flipped[0:BAND]
            turned[pl.ds(i + 8, BAND, stride=OWN), :] = flipped[BAND : 2 * BAND]
        outbox[h] = turned[...].astype(jnp.bfloat16)

    a_copies = []

    def send_chan(h):
        mine = pltpu.make_async_copy(
            outbox.at[h, pl.ds(pl.multiple_of(chan * UNIT, UNIT), UNIT), :],
            spectra.at[h, chan, feed],
            own_sem.at[h],
        )
        mine.start()
        for n, ((half, d), across) in enumerate(plane):
            other = plane_peer(half, d)
            copy = pltpu.make_async_remote_copy(
                src_ref=outbox.at[h, pl.ds(pl.multiple_of(other * UNIT, UNIT), UNIT), :],
                dst_ref=spectra.at[h, chan, feed],
                send_sem=a_send.at[h, n],
                recv_sem=a_recv.at[h, across, half],
                device_id=(other, feed_at(0, bool(across))),
                device_id_type=MESH,
            )
            copy.start()
            a_copies.append(copy)
        return mine

    def arrived(h, across, half):
        count = SUB - 1 if (across, half) == (0, 0) else SUB
        rows = spectra.at[h, pl.ds(0, count), 0]
        pltpu.make_async_copy(rows, rows, a_recv.at[h, across, half]).wait()

    sub_of = [chan // SUB, 1 - chan // SUB]

    def spread(h, n, kind, origin, target):
        block = spectra.at[h, pl.ds(pl.multiple_of(sub_of[n] * SUB, SUB), SUB), origin]
        return pltpu.make_async_remote_copy(
            src_ref=block,
            dst_ref=block,
            send_sem=b_send.at[h, kind, n],
            recv_sem=b_recv.at[h, kind, n],
            device_id=target,
            device_id_type=MESH,
        )

    plans = []
    for n in range(SUBS):
        fore, back, s = (right, left, 1) if n == 0 else (left, right, -1)
        plans.append(
            {
                "own fore": (feed, fore),
                "own back": (feed, back),
                "pass fore": (feed_at(-s, False), fore),
                "pass over": (feed_at(s, False), over),
                "other fore": (feed_at(0, True), fore),
                "other back": (feed_at(s, True), back),
            }
        )
    kinds = list(plans[0])
    made = {}

    def start(h, n, kind):
        origin, target = plans[n][kind]
        made[h, n, kind] = spread(h, n, kinds.index(kind), origin, target)
        made[h, n, kind].start()

    def landed(h, n, kind):
        made[h, n, kind].wait_recv()

    def step_one(h, n, mine):
        if n == 0:
            mine.wait()
        arrived(h, 0, n)
        start(h, n, "own back")
        start(h, n, "own fore")
        arrived(h, 1, n)
        start(h, n, "other fore")

    def step_two(h, n):
        landed(h, n, "own back")
        start(h, n, "pass over")
        landed(h, n, "own fore")
        start(h, n, "pass fore")

    def step_three(h, n):
        landed(h, n, "pass over")
        start(h, n, "other back")

    loaded(0)
    tab_copy.wait()
    convolve(0, 34)
    loaded(1)
    convolve(34, 34)
    turn(0)
    mine0 = send_chan(0)
    loaded(2)
    convolve(67, 33)
    loaded(3)
    convolve(100, 31)
    step_one(0, 0, mine0)
    turn(1)
    mine1 = send_chan(1)
    step_one(0, 1, mine0)

    sums = jnp.sum(power_acc[...], axis=1)
    first = jnp.sum(jnp.where(low8, sums, 0.0), axis=1, keepdims=True)
    second = jnp.sum(jnp.where(low8, 0.0, sums), axis=1, keepdims=True)
    column = jnp.concatenate([first, second], axis=0)
    lane16 = lax.broadcasted_iota(jnp.int32, (OWN, 128), 1)
    sub16 = lax.broadcasted_iota(jnp.int32, (OWN, 128), 0)
    power_row[...] = jnp.sum(
        jnp.where(lax.rem(lane16, OWN) == sub16, column, 0.0), axis=0, keepdims=True
    )
    p_own = pltpu.make_async_copy(power_row, powers.at[feed, chan], own_sem.at[2])
    p_own.start()
    p_copies = []
    for d in range(1, CHAN_DEVS):
        copy = pltpu.make_async_remote_copy(
            src_ref=power_row,
            dst_ref=powers.at[feed, chan],
            send_sem=p_send.at[d],
            recv_sem=p_recv.at[d],
            device_id=(lax.rem(chan + d, CHAN_DEVS), feed),
            device_id_type=MESH,
        )
        copy.start()
        p_copies.append(copy)

    step_one(1, 0, mine1)
    step_one(1, 1, mine1)

    for copy in steer_copies:
        copy.wait()
    own_steer.wait()
    flag_copy.wait()
    for g in range(FEED_DEVS):
        cols = pl.ds(g * FEED_INPUTS, FEED_INPUTS)
        index = steer_in[g].astype(jnp.float32)
        quarter = jnp.floor((index + 32.0) * (1.0 / 64.0))
        angle = (index - 64.0 * quarter) * (2.0 * np.pi / PHASES)
        sq = angle * angle
        cos = 1.0 + sq * (-1.0 / 2 + sq * (1.0 / 24 + sq * (-1.0 / 720 + sq * (1.0 / 40320))))
        sin = angle * (
            1.0 + sq * (-1.0 / 6 + sq * (1.0 / 120 + sq * (-1.0 / 5040 + sq * (1.0 / 362880))))
        )
        swap = (quarter == 1.0) | (quarter == 3.0)
        cos_neg = (quarter == 1.0) | (quarter == 2.0)
        sin_neg = (quarter == 2.0) | (quarter == 3.0)
        cos_mag = jnp.where(swap, sin, cos)
        sin_mag = jnp.where(swap, cos, sin)
        good = flag_buf[:, cols].astype(jnp.float32)
        weight_buf[0:OWN_BEAMS, cols] = (jnp.where(cos_neg, -cos_mag, cos_mag) * good).astype(
            jnp.bfloat16
        )
        weight_buf[OWN_BEAMS : 2 * OWN_BEAMS, cols] = (
            jnp.where(sin_neg, -sin_mag, sin_mag) * good
        ).astype(jnp.bfloat16)

    weight_copy = pltpu.make_async_copy(weight_buf, weights, out_sem)
    weight_copy.start()

    for h in range(2):
        for n in range(SUBS):
            step_two(h, n)

    p_own.wait()
    for copy in p_copies:
        copy.wait()
    q_copies = []
    for d in range(1, FEED_DEVS):
        copy = pltpu.make_async_remote_copy(
            src_ref=powers.at[feed],
            dst_ref=powers.at[feed],
            send_sem=q_send.at[d],
            recv_sem=q_recv.at[d],
            device_id=(chan, lax.rem(feed + d, FEED_DEVS)),
            device_id_type=MESH,
        )
        copy.start()
        q_copies.append(copy)

    for h in range(2):
        for n in range(SUBS):
            step_three(h, n)

    for copy in a_copies:
        copy.wait_send()
    for copy in q_copies:
        copy.wait()
    weight_copy.wait()
    for h in range(2):
        for n in range(SUBS):
            for kind in ("other fore", "pass fore", "other back"):
                landed(h, n, kind)
    for copy in made.values():
        copy.wait_send()


def correlate_kernel(
    spectra, powers, flags, weights, vis, beam,
    block, power_buf, flag_buf, weight_buf, product, col_scale, row_scale,
    in_sem, small_sem, out_sem,
):
    feed = lax.axis_index("feed")
    power_copy = pltpu.make_async_copy(powers, power_buf, small_sem.at[0])
    flag_copy = pltpu.make_async_copy(flags, flag_buf, small_sem.at[1])
    weight_copy = pltpu.make_async_copy(weights, weight_buf, small_sem.at[2])

    def loads(c):
        rows = pl.ds(pl.multiple_of(c * OWN, OWN), OWN)
        step = CHAN_DEVS // IN_PARTS
        return [
            pltpu.make_async_copy(
                spectra.at[h, pl.ds(n * step, step), :, rows, :],
                block.at[c, h, pl.ds(n * step, step)],
                in_sem.at[c],
            )
            for n in range(IN_PARTS)
            for h in range(2)
        ]

    power_copy.start()
    flag_copy.start()
    for c in range(PER_CHAN):
        for copy in loads(c):
            copy.start()
    weight_copy.start()
    power_copy.wait()
    flag_copy.wait()
    lane = lax.broadcasted_iota(jnp.int32, (CHAN_DEVS, 128), 1)
    power = jnp.zeros((CHAN_DEVS, 128), jnp.float32)
    for f in range(FEED_DEVS):
        power = jnp.where(lane // OWN == f, power_buf[f].reshape(CHAN_DEVS, 128), power)
    scale = lax.rsqrt(power / (BAND * NT) + EPSILON)
    col_scale[...] = scale * flag_buf[...].astype(jnp.float32)
    for n in range(2):
        one = col_scale[pl.ds(2 * feed + n, 1), :] * (1.0 / NT)
        row_scale[128 * n : 128 * (n + 1), :] = jnp.broadcast_to(one, (128, 128)).T

    def parts(c, first, count):
        return jnp.concatenate(
            [block[c, h, pl.ds(first, count)].reshape(count * 128, 128) for h in range(2)],
            axis=1,
        )

    def swapped(c, h):
        own = block[c, h, pl.ds(2 * feed, 2)].reshape(256, 128).astype(jnp.float32)
        lane = lax.broadcasted_iota(jnp.int32, (256, 128), 1)
        turned = pltpu.roll(own, HALF_T, 1)
        return jnp.where(lane < HALF_T, turned, -turned).astype(jnp.bfloat16)

    def stores(c):
        copies = []
        step = FEED_INPUTS // OUT_PARTS
        for p in range(2):
            for n in range(OUT_PARTS):
                rows = pl.ds(n * step, step)
                copies.append(
                    pltpu.make_async_copy(
                        product.at[p, c, rows, :], vis.at[p, c, rows, :], out_sem.at[c]
                    )
                )
        return copies

    @pl.loop(0, PER_CHAN)
    def _(c):
        pltpu.make_async_copy(block.at[c], block.at[c], in_sem.at[c]).wait()

        own = parts(c, 2 * feed, 2)
        turned = jnp.concatenate([swapped(c, 0), swapped(c, 1)], axis=1)
        left = jnp.concatenate([own, turned], axis=0)
        rows = row_scale[...]
        for n in range(INPUTS // 256):
            both = lax.dot_general(
                left,
                parts(c, 2 * n, 2),
                (((1,), (1,)), ((), ())),
                preferred_element_type=jnp.float32,
            )
            for m in range(2):
                scale = rows * col_scale[2 * n + m : 2 * n + m + 1, :]
                out = pl.ds((2 * n + m) * 128, 128)
                product[0, c, :, out] = both[0:256, 128 * m : 128 * (m + 1)] * scale
                product[1, c, :, out] = both[256:512, 128 * m : 128 * (m + 1)] * scale
        for copy in stores(c):
            copy.start()

    weight_copy.wait()
    lane = lax.broadcasted_iota(jnp.int32, (OWN_BEAMS, 128), 1)
    for c in range(PER_CHAN):
        sums = jnp.dot(
            weight_buf[...], parts(c, 0, CHAN_DEVS), preferred_element_type=jnp.float32
        )
        halves = []
        for h in range(2):
            cols = slice(128 * h, 128 * (h + 1))
            cos_part = sums[0:OWN_BEAMS, cols]
            sin_part = pltpu.roll(sums[OWN_BEAMS : 2 * OWN_BEAMS, cols], HALF_T, 1)
            field = cos_part + jnp.where(lane < HALF_T, -sin_part, sin_part)
            square = field * field
            halves.append(square + pltpu.roll(square, HALF_T, 1))
        beam[:, c, :] = jnp.where(lane < HALF_T, halves[0], halves[1]) * (1.0 / INPUTS)
    for c in range(PER_CHAN):
        whole = product.at[:, c]
        pltpu.make_async_copy(whole, whole, out_sem.at[c]).wait()


def channelize_turn(table, raw_volts, channel_gains, feed_flags, steer_index):
    hbm = pl.BlockSpec(memory_space=pl.ANY)
    bf16, f32 = jnp.bfloat16, jnp.float32
    dma = pltpu.SemaphoreType.DMA
    spectra, powers, weights = pl.pallas_call(
        turn_kernel,
        name="channelize_turn",
        out_shape=(
            jax.ShapeDtypeStruct((2, CHAN_DEVS, FEED_DEVS, UNIT, 128), bf16),
            jax.ShapeDtypeStruct((FEED_DEVS, CHAN_DEVS, 1, 128), f32),
            jax.ShapeDtypeStruct((2 * OWN_BEAMS, INPUTS), bf16),
        ),
        in_specs=[hbm] * 5,
        out_specs=(hbm, hbm, hbm),
        scratch_shapes=[
            pltpu.VMEM((SLABS * OWN, BLOCK), bf16),
            pltpu.VMEM((BLOCK, TAPS * 128), bf16),
            pltpu.VMEM((SLABS * OWN, TAPS * 128), f32),
            pltpu.VMEM((HALF_T * OWN, 128), f32),
            pltpu.VMEM((BAND * OWN, 128), f32),
            pltpu.VMEM((2, BAND * OWN, 128), bf16),
            pltpu.VMEM((2, OWN, BAND), f32),
            pltpu.VMEM((BEAMS, FEED_INPUTS), jnp.int32),
            pltpu.VMEM((1, INPUTS), jnp.int32),
            pltpu.VMEM((8, 8, 128), f32),
            pltpu.VMEM((1, 128), f32),
            pltpu.VMEM((BEAMS, FEED_INPUTS), bf16),
            pltpu.VMEM((FEED_DEVS, OWN_BEAMS, FEED_INPUTS), bf16),
            pltpu.VMEM((2 * OWN_BEAMS, INPUTS), bf16),
            dma((4,)),
            dma,
            dma((3,)),
            dma((3,)),
            dma((2, 2 * CHAN_DEVS)),
            dma((2, 2, SUBS)),
            dma((2, KINDS, SUBS)),
            dma((2, KINDS, SUBS)),
            dma((FEED_DEVS,)),
            dma((FEED_DEVS,)),
            dma((CHAN_DEVS,)),
            dma((CHAN_DEVS,)),
            dma((FEED_DEVS,)),
            dma((FEED_DEVS,)),
            dma,
        ],
        compiler_params=pltpu.CompilerParams(
            collective_id=0, has_side_effects=True, vmem_limit_bytes=60 * 2**20
        ),
        cost_estimate=pl.CostEstimate(
            flops=2 * SLABS * OWN * BLOCK * 512, bytes_accessed=20_000_000, transcendentals=0
        ),
    )(raw_volts, table, jnp.transpose(channel_gains, (0, 2, 1)), steer_index, feed_flags.reshape(1, INPUTS))
    return spectra, powers, weights


def correlate(spectra, powers, feed_flags, weights):
    bf16, f32 = jnp.bfloat16, jnp.float32
    hbm = pl.BlockSpec(memory_space=pl.ANY)
    vmem = pl.BlockSpec(memory_space=pltpu.VMEM)
    dma = pltpu.SemaphoreType.DMA
    return pl.pallas_call(
        correlate_kernel,
        name="correlate",
        out_shape=(
            jax.ShapeDtypeStruct((2, PER_CHAN, FEED_INPUTS, INPUTS), f32),
            jax.ShapeDtypeStruct((OWN_BEAMS, PER_CHAN, NT), f32),
        ),
        in_specs=[hbm] * 4,
        out_specs=(hbm, vmem),
        scratch_shapes=[
            pltpu.VMEM((PER_CHAN, 2, CHAN_DEVS, FEED_DEVS, OWN, 128), bf16),
            pltpu.VMEM((FEED_DEVS, CHAN_DEVS, 1, 128), f32),
            pltpu.VMEM((CHAN_DEVS, 128), jnp.int32),
            pltpu.VMEM((2 * OWN_BEAMS, INPUTS), bf16),
            pltpu.VMEM((2, PER_CHAN, FEED_INPUTS, INPUTS), f32),
            pltpu.VMEM((CHAN_DEVS, 128), f32),
            pltpu.VMEM((256, 128), f32),
            dma((PER_CHAN,)),
            dma((3,)),
            dma((PER_CHAN,)),
        ],
        compiler_params=pltpu.CompilerParams(vmem_limit_bytes=60 * 2**20),
        cost_estimate=pl.CostEstimate(
            flops=2_700_000_000, bytes_accessed=22_000_000, transcendentals=0
        ),
    )(spectra, powers, feed_flags.reshape(CHAN_DEVS, 128), weights)


def solution(mesh):
    table = filter_table()
    in_specs = (P(("chan", "feed"), None), P(None, None, ("chan", "feed")), P(), P(None, "feed"))
    out_specs = (P(None, "chan", "feed", None), P("feed", "chan", None))

    def body(raw_volts, channel_gains, feed_flags, steer_index):
        spectra, powers, weights = channelize_turn(
            jnp.asarray(table), raw_volts, channel_gains, feed_flags, steer_index
        )
        return correlate(spectra, powers, feed_flags, weights)

    return jax.shard_map(
        body, mesh=mesh, in_specs=in_specs, out_specs=out_specs, check_vma=False
    )
```

```python
import functools

import jax
import jax.numpy as jnp
import ml_dtypes
import numpy as np
from jax import lax
from jax.experimental import pallas as pl
from jax.experimental.pallas import tpu as pltpu
from jax.sharding import PartitionSpec as P

CHANS = 1024
INPUTS = 2048
TAPS = 4
PHASES = 256
NT = 128
BAND = 64
BEAMS = 512
BLOCK = 2 * CHANS
EPSILON = 1e-06

CHAN_DEVS = 16
FEED_DEVS = 8
OWN = 16
PER_CHAN = BAND // CHAN_DEVS
UNIT = PER_CHAN * OWN
HALF_T = NT // 2
SLABS = NT + TAPS - 1
SUBS = 2
SUB = CHAN_DEVS // SUBS
OWN_BEAMS = BEAMS // FEED_DEVS
FEED_INPUTS = INPUTS // FEED_DEVS
KINDS = 6
OUT_PARTS = 4
MESH = pl.DeviceIdType.MESH


def filter_table():
    full_len = TAPS * BLOCK
    pos = np.arange(full_len, dtype=np.float64)
    centred = (pos + 0.5) / full_len - 0.5
    window = np.sinc(TAPS * centred) * (0.5 - 0.5 * np.cos(2.0 * np.pi * (pos + 0.5) / full_len))
    window = window / np.sqrt(np.sum(window * window))
    channel = CHANS // 2 - BAND // 2 + np.arange(BAND)
    turn = (np.arange(BLOCK)[:, None] * channel[None, :]) % BLOCK
    angle = 2.0 * np.pi / BLOCK * turn
    weights = window.reshape(TAPS, BLOCK)[:, :, None]
    table = np.concatenate([weights * np.cos(angle), -(weights * np.sin(angle))], axis=2)
    return np.transpose(table, (1, 0, 2)).reshape(BLOCK, TAPS * 2 * BAND).astype(ml_dtypes.bfloat16)


def turn_kernel(
    raw, table, gains, steer, spectra, powers, weights,
    volts, tab, conv, summed, turned, outbox, gain_buf, steer_buf, power_acc, power_row,
    steer_out, steer_in, weight_buf,
    load_sem, tab_sem, small_sem, own_sem, a_send, a_recv, b_send, b_recv,
    s_send, s_recv, p_send, p_recv, q_send, q_recv, out_sem,
):
    chan = lax.axis_index("chan")
    feed = lax.axis_index("feed")
    x = feed // 2
    row = feed % 2

    def feed_at(dx, across):
        r = 1 - row if across else row
        return lax.rem(x + dx + 4, 4) * 2 + r

    right = (chan, feed_at(1, False))
    left = (chan, feed_at(-1, False))
    over = (chan, feed_at(0, True))

    barrier = pltpu.get_barrier_semaphore()
    plane = [
        ((half, d), across)
        for half in range(SUBS)
        for across in range(2)
        for d in range(SUB)
        if (half, d, across) != (0, 0, 0)
    ]

    def plane_peer(half, d):
        first = (chan // SUB + half) % SUBS * SUB
        return first + lax.rem(chan + d, SUB)

    distant = [(dx, across) for dx in (1, 3, 2) for across in (False, True)]
    for (half, d), across in plane:
        pl.semaphore_signal(
            barrier,
            inc=1,
            device_id=(plane_peer(half, d), feed_at(0, bool(across))),
            device_id_type=MESH,
        )
    for dx, across in distant:
        pl.semaphore_signal(
            barrier, inc=1, device_id=(chan, feed_at(dx, across)), device_id_type=MESH
        )

    tab_copy = pltpu.make_async_copy(table.at[0], tab, tab_sem)
    tab_copy.start()
    gain_copy = pltpu.make_async_copy(gains, gain_buf, small_sem.at[0])
    gain_copy.start()
    steer_copy = pltpu.make_async_copy(steer, steer_buf, small_sem.at[1])
    steer_copy.start()
    groups = [(0, 34), (34, 34), (68, 32), (100, 31)]
    for g, (first, count) in enumerate(groups):

        @pl.loop(0, count)
        def _(n):
            s = first + n
            pltpu.make_async_copy(
                raw.at[:, pl.ds(pl.multiple_of(s * BLOCK, BLOCK), BLOCK)],
                volts.at[pl.ds(pl.multiple_of(s * OWN, OWN), OWN), :],
                load_sem.at[g],
            ).start()

    gain_copy.wait()
    pair_re = jnp.concatenate([gain_buf[0, 0:8], gain_buf[0, 8:16]], axis=1)
    pair_im = jnp.concatenate([gain_buf[1, 0:8], gain_buf[1, 8:16]], axis=1)
    lane8 = lax.broadcasted_iota(jnp.int32, (8, 128), 1)
    low8 = lane8 < BAND

    low = lax.broadcasted_iota(jnp.int32, (HALF_T, 128), 1) < BAND

    def loaded(g):
        first, count = groups[g]
        rows = volts.at[pl.ds(first * OWN, count * OWN), :]
        pltpu.make_async_copy(rows, rows, load_sem.at[g]).wait()

    def convolve(first, count):
        conv[pl.ds(first * OWN, count * OWN), :] = jnp.dot(
            volts[pl.ds(first * OWN, count * OWN), :], tab[...], preferred_element_type=jnp.float32
        )

    def turn(h):
        total = None
        for k in range(TAPS):
            part = conv[pl.ds((HALF_T * h + k) * OWN, HALF_T * OWN), 128 * k : 128 * (k + 1)]
            total = part if total is None else total + part
        summed[...] = total
        for i in range(8):
            a = summed[pl.ds(i, HALF_T, stride=OWN), :]
            b = summed[pl.ds(i + 8, HALF_T, stride=OWN), :]
            re = jnp.where(low, a, pltpu.roll(b, BAND, 1))
            im = jnp.where(low, pltpu.roll(a, BAND, 1), b)
            g_re = pair_re[i : i + 1]
            g_im = pair_im[i : i + 1]
            spec_re = (g_re * re - g_im * im).astype(jnp.bfloat16).astype(jnp.float32)
            spec_im = (g_re * im + g_im * re).astype(jnp.bfloat16).astype(jnp.float32)
            power = spec_re * spec_re + spec_im * spec_im
            power = jnp.sum(power.reshape(HALF_T // 8, 8, 128), axis=0)
            if h == 0:
                power_acc[i] = power
            else:
                power_acc[i] = power_acc[i] + power
            flipped = jnp.concatenate([spec_re, spec_im], axis=0).T
            turned[pl.ds(i, BAND, stride=OWN), :] = flipped[0:BAND]
            turned[pl.ds(i + 8, BAND, stride=OWN), :] = flipped[BAND : 2 * BAND]
        outbox[h] = turned[...].astype(jnp.bfloat16)

    a_copies = []

    def send_chan(h):
        mine = pltpu.make_async_copy(
            outbox.at[h, pl.ds(pl.multiple_of(chan * UNIT, UNIT), UNIT), :],
            spectra.at[h, chan, feed],
            own_sem.at[h],
        )
        mine.start()
        for n, ((half, d), across) in enumerate(plane):
            other = plane_peer(half, d)
            copy = pltpu.make_async_remote_copy(
                src_ref=outbox.at[h, pl.ds(pl.multiple_of(other * UNIT, UNIT), UNIT), :],
                dst_ref=spectra.at[h, chan, feed],
                send_sem=a_send.at[h, n],
                recv_sem=a_recv.at[h, across, half],
                device_id=(other, feed_at(0, bool(across))),
                device_id_type=MESH,
            )
            copy.start()
            a_copies.append(copy)
        return mine

    def arrived(h, across, half):
        count = SUB - 1 if (across, half) == (0, 0) else SUB
        rows = spectra.at[h, pl.ds(0, count), 0]
        pltpu.make_async_copy(rows, rows, a_recv.at[h, across, half]).wait()

    sub_of = [chan // SUB, 1 - chan // SUB]

    def spread(h, n, kind, origin, target):
        block = spectra.at[h, pl.ds(pl.multiple_of(sub_of[n] * SUB, SUB), SUB), origin]
        return pltpu.make_async_remote_copy(
            src_ref=block,
            dst_ref=block,
            send_sem=b_send.at[h, kind, n],
            recv_sem=b_recv.at[h, kind, n],
            device_id=target,
            device_id_type=MESH,
        )

    plans = []
    for n in range(SUBS):
        fore, back, s = (right, left, 1) if n == 0 else (left, right, -1)
        plans.append(
            {
                "own fore": (feed, fore),
                "own back": (feed, back),
                "pass fore": (feed_at(-s, False), fore),
                "pass over": (feed_at(s, False), over),
                "other fore": (feed_at(0, True), fore),
                "other back": (feed_at(s, True), back),
            }
        )
    kinds = list(plans[0])
    made = {}

    def start(h, n, kind):
        origin, target = plans[n][kind]
        made[h, n, kind] = spread(h, n, kinds.index(kind), origin, target)
        made[h, n, kind].start()

    def landed(h, n, kind):
        made[h, n, kind].wait_recv()

    def step_one(h, n, mine):
        if n == 0:
            mine.wait()
        arrived(h, 0, n)
        start(h, n, "own back")
        start(h, n, "own fore")
        arrived(h, 1, n)
        start(h, n, "other fore")

    def step_two(h, n):
        landed(h, n, "own back")
        start(h, n, "pass over")
        landed(h, n, "own fore")
        start(h, n, "pass fore")

    def step_three(h, n):
        landed(h, n, "pass over")
        start(h, n, "other back")

    loaded(0)
    tab_copy.wait()
    convolve(0, 34)

    steer_copy.wait()
    steer_out[...] = steer_buf[...].astype(jnp.float32).astype(jnp.bfloat16)
    pl.semaphore_wait(barrier, len(plane) + len(distant))
    steer_copies = []
    for d in range(1, FEED_DEVS):
        other = lax.rem(feed + d, FEED_DEVS)
        steer_copies.append(
            pltpu.make_async_remote_copy(
                src_ref=steer_out.at[pl.ds(pl.multiple_of(other * OWN_BEAMS, OWN_BEAMS), OWN_BEAMS), :],
                dst_ref=steer_in.at[feed],
                send_sem=s_send.at[d],
                recv_sem=s_recv.at[d],
                device_id=(chan, other),
                device_id_type=MESH,
            )
        )
        steer_copies[-1].start()
    own_steer = pltpu.make_async_copy(
        steer_out.at[pl.ds(pl.multiple_of(feed * OWN_BEAMS, OWN_BEAMS), OWN_BEAMS), :],
        steer_in.at[feed],
        s_send.at[0],
    )
    own_steer.start()

    loaded(1)
    convolve(34, 34)
    turn(0)
    mine0 = send_chan(0)
    loaded(2)
    convolve(67, 33)
    loaded(3)
    convolve(100, 31)
    step_one(0, 0, mine0)
    turn(1)
    mine1 = send_chan(1)
    step_one(0, 1, mine0)

    sums = jnp.sum(power_acc[...], axis=1)
    first = jnp.sum(jnp.where(low8, sums, 0.0), axis=1, keepdims=True)
    second = jnp.sum(jnp.where(low8, 0.0, sums), axis=1, keepdims=True)
    column = jnp.concatenate([first, second], axis=0)
    lane16 = lax.broadcasted_iota(jnp.int32, (OWN, 128), 1)
    sub16 = lax.broadcasted_iota(jnp.int32, (OWN, 128), 0)
    power_row[...] = jnp.sum(
        jnp.where(lax.rem(lane16, OWN) == sub16, column, 0.0), axis=0, keepdims=True
    )
    p_own = pltpu.make_async_copy(power_row, powers.at[feed, chan], own_sem.at[2])
    p_own.start()
    p_copies = []
    for d in range(1, CHAN_DEVS):
        copy = pltpu.make_async_remote_copy(
            src_ref=power_row,
            dst_ref=powers.at[feed, chan],
            send_sem=p_send.at[d],
            recv_sem=p_recv.at[d],
            device_id=(lax.rem(chan + d, CHAN_DEVS), feed),
            device_id_type=MESH,
        )
        copy.start()
        p_copies.append(copy)

    step_two(0, 0)
    step_one(1, 0, mine1)
    step_two(0, 1)
    step_one(1, 1, mine1)

    for copy in steer_copies:
        copy.wait()
    own_steer.wait()
    for g in range(FEED_DEVS):
        cols = pl.ds(g * FEED_INPUTS, FEED_INPUTS)
        index = steer_in[g].astype(jnp.float32)
        quarter = jnp.floor((index + 32.0) * (1.0 / 64.0))
        angle = (index - 64.0 * quarter) * (2.0 * np.pi / PHASES)
        sq = angle * angle
        cos = 1.0 + sq * (-1.0 / 2 + sq * (1.0 / 24 + sq * (-1.0 / 720 + sq * (1.0 / 40320))))
        sin = angle * (
            1.0 + sq * (-1.0 / 6 + sq * (1.0 / 120 + sq * (-1.0 / 5040 + sq * (1.0 / 362880))))
        )
        swap = (quarter == 1.0) | (quarter == 3.0)
        cos_neg = (quarter == 1.0) | (quarter == 2.0)
        sin_neg = (quarter == 2.0) | (quarter == 3.0)
        cos_mag = jnp.where(swap, sin, cos)
        sin_mag = jnp.where(swap, cos, sin)
        weight_buf[0:OWN_BEAMS, cols] = jnp.where(cos_neg, -cos_mag, cos_mag).astype(jnp.bfloat16)
        weight_buf[OWN_BEAMS : 2 * OWN_BEAMS, cols] = jnp.where(sin_neg, -sin_mag, sin_mag).astype(
            jnp.bfloat16
        )

    weight_copy = pltpu.make_async_copy(weight_buf, weights, out_sem)
    weight_copy.start()

    step_two(1, 0)
    step_two(1, 1)

    p_own.wait()
    for copy in p_copies:
        copy.wait()
    q_copies = []
    for d in range(1, FEED_DEVS):
        copy = pltpu.make_async_remote_copy(
            src_ref=powers.at[feed],
            dst_ref=powers.at[feed],
            send_sem=q_send.at[d],
            recv_sem=q_recv.at[d],
            device_id=(chan, lax.rem(feed + d, FEED_DEVS)),
            device_id_type=MESH,
        )
        copy.start()
        q_copies.append(copy)

    for h in range(2):
        for n in range(SUBS):
            step_three(h, n)

    for copy in a_copies:
        copy.wait_send()
    for copy in q_copies:
        copy.wait()
    weight_copy.wait()
    for h in range(2):
        for n in range(SUBS):
            for kind in ("other fore", "pass fore", "other back"):
                landed(h, n, kind)
    for copy in made.values():
        copy.wait_send()


def correlate_kernel(
    spectra, powers, flags, flag_row, weights, vis, beam,
    product, col_scale, row_scale, out_sem,
):
    feed = lax.axis_index("feed")
    lane = lax.broadcasted_iota(jnp.int32, (CHAN_DEVS, 128), 1)
    power = jnp.zeros((CHAN_DEVS, 128), jnp.float32)
    for f in range(FEED_DEVS):
        power = jnp.where(lane // OWN == f, powers[f].reshape(CHAN_DEVS, 128), power)
    scale = lax.rsqrt(power / (BAND * NT) + EPSILON)
    col_scale[...] = scale * flags[...].astype(jnp.float32)
    for n in range(2):
        one = col_scale[pl.ds(2 * feed + n, 1), :] * (1.0 / NT)
        row_scale[128 * n : 128 * (n + 1), :] = jnp.broadcast_to(one, (128, 128)).T

    def parts(c, first, count):
        return jnp.concatenate(
            [
                spectra[h, pl.ds(first, count), :, pl.ds(c * OWN, OWN), :].reshape(count * 128, 128)
                for h in range(2)
            ],
            axis=1,
        )

    def swapped(c, h):
        own = spectra[h, pl.ds(2 * feed, 2), :, pl.ds(c * OWN, OWN), :]
        own = own.reshape(256, 128).astype(jnp.float32)
        lane = lax.broadcasted_iota(jnp.int32, (256, 128), 1)
        turned = pltpu.roll(own, HALF_T, 1)
        return jnp.where(lane < HALF_T, turned, -turned).astype(jnp.bfloat16)

    def stores(c):
        copies = []
        step = FEED_INPUTS // OUT_PARTS
        for p in range(2):
            for n in range(OUT_PARTS):
                rows = pl.ds(n * step, step)
                copies.append(
                    pltpu.make_async_copy(
                        product.at[p, c, rows, :], vis.at[p, c, rows, :], out_sem.at[c]
                    )
                )
        return copies

    @pl.loop(0, PER_CHAN)
    def _(c):

        own = parts(c, 2 * feed, 2)
        turned = jnp.concatenate([swapped(c, 0), swapped(c, 1)], axis=1)
        left = jnp.concatenate([own, turned], axis=0)
        rows = row_scale[...]
        for n in range(INPUTS // 256):
            both = lax.dot_general(
                left,
                parts(c, 2 * n, 2),
                (((1,), (1,)), ((), ())),
                preferred_element_type=jnp.float32,
            )
            for m in range(2):
                scale = rows * col_scale[2 * n + m : 2 * n + m + 1, :]
                out = pl.ds((2 * n + m) * 128, 128)
                product[0, c, :, out] = both[0:256, 128 * m : 128 * (m + 1)] * scale
                product[1, c, :, out] = both[256:512, 128 * m : 128 * (m + 1)] * scale
        for copy in stores(c):
            copy.start()

    good = weights[...] * flag_row[...].astype(jnp.float32).astype(jnp.bfloat16)
    lane = lax.broadcasted_iota(jnp.int32, (OWN_BEAMS, 128), 1)
    for c in range(PER_CHAN):
        sums = jnp.dot(
            good, parts(c, 0, CHAN_DEVS), preferred_element_type=jnp.float32
        )
        halves = []
        for h in range(2):
            cols = slice(128 * h, 128 * (h + 1))
            cos_part = sums[0:OWN_BEAMS, cols]
            sin_part = pltpu.roll(sums[OWN_BEAMS : 2 * OWN_BEAMS, cols], HALF_T, 1)
            field = cos_part + jnp.where(lane < HALF_T, -sin_part, sin_part)
            square = field * field
            halves.append(square + pltpu.roll(square, HALF_T, 1))
        beam[:, c, :] = jnp.where(lane < HALF_T, halves[0], halves[1]) * (1.0 / INPUTS)
    for c in range(PER_CHAN):
        whole = product.at[:, c]
        pltpu.make_async_copy(whole, whole, out_sem.at[c]).wait()


def channelize_turn(table, raw_volts, channel_gains, steer_index):
    hbm = pl.BlockSpec(memory_space=pl.ANY)
    bf16, f32 = jnp.bfloat16, jnp.float32
    dma = pltpu.SemaphoreType.DMA
    spectra, powers, weights = pl.pallas_call(
        turn_kernel,
        name="channelize_turn",
        out_shape=(
            jax.ShapeDtypeStruct((2, CHAN_DEVS, FEED_DEVS, UNIT, 128), bf16),
            jax.ShapeDtypeStruct((FEED_DEVS, CHAN_DEVS, 1, 128), f32),
            jax.ShapeDtypeStruct((2 * OWN_BEAMS, INPUTS), bf16),
        ),
        in_specs=[hbm] * 4,
        out_specs=(hbm, hbm, hbm),
        scratch_shapes=[
            pltpu.VMEM((SLABS * OWN, BLOCK), bf16),
            pltpu.VMEM((BLOCK, TAPS * 128), bf16),
            pltpu.VMEM((SLABS * OWN, TAPS * 128), f32),
            pltpu.VMEM((HALF_T * OWN, 128), f32),
            pltpu.VMEM((BAND * OWN, 128), f32),
            pltpu.VMEM((2, BAND * OWN, 128), bf16),
            pltpu.VMEM((2, OWN, BAND), f32),
            pltpu.VMEM((BEAMS, FEED_INPUTS), jnp.int32),
            pltpu.VMEM((8, 8, 128), f32),
            pltpu.VMEM((1, 128), f32),
            pltpu.VMEM((BEAMS, FEED_INPUTS), bf16),
            pltpu.VMEM((FEED_DEVS, OWN_BEAMS, FEED_INPUTS), bf16),
            pltpu.VMEM((2 * OWN_BEAMS, INPUTS), bf16),
            dma((4,)),
            dma,
            dma((3,)),
            dma((3,)),
            dma((2, 2 * CHAN_DEVS)),
            dma((2, 2, SUBS)),
            dma((2, KINDS, SUBS)),
            dma((2, KINDS, SUBS)),
            dma((FEED_DEVS,)),
            dma((FEED_DEVS,)),
            dma((CHAN_DEVS,)),
            dma((CHAN_DEVS,)),
            dma((FEED_DEVS,)),
            dma((FEED_DEVS,)),
            dma,
        ],
        compiler_params=pltpu.CompilerParams(
            collective_id=0, has_side_effects=True, vmem_limit_bytes=46000 * 1024
        ),
        cost_estimate=pl.CostEstimate(
            flops=2 * SLABS * OWN * BLOCK * 512, bytes_accessed=20_000_000, transcendentals=0
        ),
    )(raw_volts, table, jnp.transpose(channel_gains, (0, 2, 1)), steer_index)
    return spectra, powers, weights


def correlate(spectra, powers, feed_flags, weights):
    f32 = jnp.float32
    hbm = pl.BlockSpec(memory_space=pl.ANY)
    vmem = pl.BlockSpec(memory_space=pltpu.VMEM)
    dma = pltpu.SemaphoreType.DMA
    return pl.pallas_call(
        correlate_kernel,
        name="correlate",
        out_shape=(
            jax.ShapeDtypeStruct((2, PER_CHAN, FEED_INPUTS, INPUTS), f32),
            jax.ShapeDtypeStruct((OWN_BEAMS, PER_CHAN, NT), f32),
        ),
        in_specs=[vmem] * 5,
        out_specs=(hbm, vmem),
        scratch_shapes=[
            pltpu.VMEM((2, PER_CHAN, FEED_INPUTS, INPUTS), f32),
            pltpu.VMEM((CHAN_DEVS, 128), f32),
            pltpu.VMEM((256, 128), f32),
            dma((PER_CHAN,)),
        ],
        compiler_params=pltpu.CompilerParams(vmem_limit_bytes=28 * 2**20),
        cost_estimate=pl.CostEstimate(
            flops=2_700_000_000, bytes_accessed=22_000_000, transcendentals=0
        ),
    )(spectra, powers, feed_flags.reshape(CHAN_DEVS, 128), feed_flags.reshape(1, INPUTS), weights)


def solution(mesh):
    table = np.stack([filter_table()] * 4)
    in_specs = (P(("chan", "feed"), None), P(None, None, ("chan", "feed")), P(), P(None, "feed"))
    out_specs = (P(None, "chan", "feed", None), P("feed", "chan", None))

    def body(raw_volts, channel_gains, feed_flags, steer_index):
        spectra, powers, weights = channelize_turn(
            jnp.asarray(table), raw_volts, channel_gains, steer_index
        )
        return correlate(spectra, powers, feed_flags, weights)

    return jax.shard_map(
        body, mesh=mesh, in_specs=in_specs, out_specs=out_specs, check_vma=False
    )
```

```python
import functools

import jax
import jax.numpy as jnp
import ml_dtypes
import numpy as np
from jax import lax
from jax.experimental import pallas as pl
from jax.experimental.pallas import tpu as pltpu
from jax.sharding import PartitionSpec as P

CHANS = 1024
INPUTS = 2048
TAPS = 4
PHASES = 256
NT = 128
BAND = 64
BEAMS = 512
BLOCK = 2 * CHANS
EPSILON = 1e-06

CHAN_DEVS = 16
FEED_DEVS = 8
OWN = 16
PER_CHAN = BAND // CHAN_DEVS
UNIT = PER_CHAN * OWN
HALF_T = NT // 2
SLABS = NT + TAPS - 1
SUBS = 4
SUB = CHAN_DEVS // SUBS
OWN_BEAMS = BEAMS // FEED_DEVS
FEED_INPUTS = INPUTS // FEED_DEVS
KINDS = 6
OUT_PARTS = 4
MESH = pl.DeviceIdType.MESH


def filter_table():
    full_len = TAPS * BLOCK
    pos = np.arange(full_len, dtype=np.float64)
    centred = (pos + 0.5) / full_len - 0.5
    window = np.sinc(TAPS * centred) * (0.5 - 0.5 * np.cos(2.0 * np.pi * (pos + 0.5) / full_len))
    window = window / np.sqrt(np.sum(window * window))
    channel = CHANS // 2 - BAND // 2 + np.arange(BAND)
    turn = (np.arange(BLOCK)[:, None] * channel[None, :]) % BLOCK
    angle = 2.0 * np.pi / BLOCK * turn
    weights = window.reshape(TAPS, BLOCK)[:, :, None]
    table = np.concatenate([weights * np.cos(angle), -(weights * np.sin(angle))], axis=2)
    return np.transpose(table, (1, 0, 2)).reshape(BLOCK, TAPS * 2 * BAND).astype(ml_dtypes.bfloat16)


def turn_kernel(
    raw, table, gains, steer, spectra, powers, weights,
    volts, tab, conv, summed, turned, outbox, gain_buf, steer_buf, power_acc, power_row,
    steer_out, steer_in, weight_buf,
    load_sem, tab_sem, small_sem, own_sem, a_send, a_recv, b_send, b_recv,
    s_send, s_recv, p_send, p_recv, q_send, q_recv, out_sem,
):
    chan = lax.axis_index("chan")
    feed = lax.axis_index("feed")
    x = feed // 2
    row = feed % 2

    def feed_at(dx, across):
        r = 1 - row if across else row
        return lax.rem(x + dx + 4, 4) * 2 + r

    right = (chan, feed_at(1, False))
    left = (chan, feed_at(-1, False))
    over = (chan, feed_at(0, True))

    barrier = pltpu.get_barrier_semaphore()
    plane = [
        ((half, d), across)
        for half in range(SUBS)
        for across in range(2)
        for d in range(SUB)
        if (half, d, across) != (0, 0, 0)
    ]

    def near(k):
        if SUBS == 2:
            return (chan // SUB + k) % 2
        return (chan // 8 + k // 2) % 2 * 2 + (chan // 4 + k) % 2

    def plane_peer(half, d):
        return near(half) * SUB + lax.rem(chan + d, SUB)

    distant = [(dx, across) for dx in (1, 3, 2) for across in (False, True)]
    for (half, d), across in plane:
        pl.semaphore_signal(
            barrier,
            inc=1,
            device_id=(plane_peer(half, d), feed_at(0, bool(across))),
            device_id_type=MESH,
        )
    for dx, across in distant:
        pl.semaphore_signal(
            barrier, inc=1, device_id=(chan, feed_at(dx, across)), device_id_type=MESH
        )

    tab_copy = pltpu.make_async_copy(table.at[0], tab, tab_sem)
    tab_copy.start()
    gain_copy = pltpu.make_async_copy(gains, gain_buf, small_sem.at[0])
    gain_copy.start()
    steer_copy = pltpu.make_async_copy(steer, steer_buf, small_sem.at[1])
    steer_copy.start()
    groups = [(0, 34), (34, 34), (68, 32), (100, 31)]

    def fetch(g):
        first, count = groups[g]

        @pl.loop(0, count)
        def _(n):
            s = first + n
            pltpu.make_async_copy(
                raw.at[:, pl.ds(pl.multiple_of(s * BLOCK, BLOCK), BLOCK)],
                volts.at[pl.ds(pl.multiple_of(s * OWN, OWN), OWN), :],
                load_sem.at[g],
            ).start()

    fetch(0)
    fetch(1)

    gain_copy.wait()
    pair_re = jnp.concatenate([gain_buf[0, 0:8], gain_buf[0, 8:16]], axis=1)
    pair_im = jnp.concatenate([gain_buf[1, 0:8], gain_buf[1, 8:16]], axis=1)
    lane8 = lax.broadcasted_iota(jnp.int32, (8, 128), 1)
    low8 = lane8 < BAND

    low = lax.broadcasted_iota(jnp.int32, (HALF_T, 128), 1) < BAND

    def loaded(g):
        first, count = groups[g]
        rows = volts.at[pl.ds(first * OWN, count * OWN), :]
        pltpu.make_async_copy(rows, rows, load_sem.at[g]).wait()

    def convolve(first, count):
        conv[pl.ds(first * OWN, count * OWN), :] = jnp.dot(
            volts[pl.ds(first * OWN, count * OWN), :], tab[...], preferred_element_type=jnp.float32
        )

    def turn(h):
        total = None
        for k in range(TAPS):
            part = conv[pl.ds((HALF_T * h + k) * OWN, HALF_T * OWN), 128 * k : 128 * (k + 1)]
            total = part if total is None else total + part
        summed[...] = total
        for i in range(8):
            a = summed[pl.ds(i, HALF_T, stride=OWN), :]
            b = summed[pl.ds(i + 8, HALF_T, stride=OWN), :]
            re = jnp.where(low, a, pltpu.roll(b, BAND, 1))
            im = jnp.where(low, pltpu.roll(a, BAND, 1), b)
            g_re = pair_re[i : i + 1]
            g_im = pair_im[i : i + 1]
            spec_re = (g_re * re - g_im * im).astype(jnp.bfloat16).astype(jnp.float32)
            spec_im = (g_re * im + g_im * re).astype(jnp.bfloat16).astype(jnp.float32)
            power = spec_re * spec_re + spec_im * spec_im
            power = jnp.sum(power.reshape(HALF_T // 8, 8, 128), axis=0)
            if h == 0:
                power_acc[i] = power
            else:
                power_acc[i] = power_acc[i] + power
            flipped = jnp.concatenate([spec_re, spec_im], axis=0).T
            turned[pl.ds(i, BAND, stride=OWN), :] = flipped[0:BAND]
            turned[pl.ds(i + 8, BAND, stride=OWN), :] = flipped[BAND : 2 * BAND]
        outbox[h] = turned[...].astype(jnp.bfloat16)

    a_copies = []

    def send_chan(h):
        mine = pltpu.make_async_copy(
            outbox.at[h, pl.ds(pl.multiple_of(chan * UNIT, UNIT), UNIT), :],
            spectra.at[h, chan, feed],
            own_sem.at[h],
        )
        mine.start()
        for n, ((half, d), across) in enumerate(plane):
            other = plane_peer(half, d)
            copy = pltpu.make_async_remote_copy(
                src_ref=outbox.at[h, pl.ds(pl.multiple_of(other * UNIT, UNIT), UNIT), :],
                dst_ref=spectra.at[h, chan, feed],
                send_sem=a_send.at[h, n],
                recv_sem=a_recv.at[h, across, half],
                device_id=(other, feed_at(0, bool(across))),
                device_id_type=MESH,
            )
            copy.start()
            a_copies.append(copy)
        return mine

    def arrived(h, across, half):
        count = SUB - 1 if (across, half) == (0, 0) else SUB
        rows = spectra.at[h, pl.ds(0, count), 0]
        pltpu.make_async_copy(rows, rows, a_recv.at[h, across, half]).wait()

    sub_of = [near(k) for k in range(SUBS)]

    def spread(h, n, kind, origin, target):
        block = spectra.at[h, pl.ds(pl.multiple_of(sub_of[n] * SUB, SUB), SUB), origin]
        return pltpu.make_async_remote_copy(
            src_ref=block,
            dst_ref=block,
            send_sem=b_send.at[h, kind, n],
            recv_sem=b_recv.at[h, kind, n],
            device_id=target,
            device_id_type=MESH,
        )

    plans = []
    for n in range(SUBS):
        fore, back, s = (right, left, 1) if n % 2 == 0 else (left, right, -1)
        plans.append(
            {
                "own fore": (feed, fore),
                "own back": (feed, back),
                "pass fore": (feed_at(-s, False), fore),
                "pass over": (feed_at(s, False), over),
                "other fore": (feed_at(0, True), fore),
                "other back": (feed_at(s, True), back),
            }
        )
    kinds = list(plans[0])
    made = {}

    def start(h, n, kind):
        origin, target = plans[n][kind]
        made[h, n, kind] = spread(h, n, kinds.index(kind), origin, target)
        made[h, n, kind].start()

    def landed(h, n, kind):
        made[h, n, kind].wait_recv()

    def step_one(h, n, mine):
        if n == 0:
            mine.wait()
        arrived(h, 0, n)
        start(h, n, "own back")
        start(h, n, "own fore")
        arrived(h, 1, n)
        start(h, n, "other fore")

    def step_two(h, n):
        landed(h, n, "own back")
        start(h, n, "pass over")
        landed(h, n, "own fore")
        start(h, n, "pass fore")

    def step_three(h, n):
        landed(h, n, "pass over")
        start(h, n, "other back")

    loaded(0)
    tab_copy.wait()
    fetch(2)
    fetch(3)
    convolve(0, 34)

    steer_copy.wait()
    steer_out[...] = steer_buf[...].astype(jnp.float32).astype(jnp.bfloat16)
    pl.semaphore_wait(barrier, len(plane) + len(distant))
    steer_copies = []
    for d in range(1, FEED_DEVS):
        other = lax.rem(feed + d, FEED_DEVS)
        steer_copies.append(
            pltpu.make_async_remote_copy(
                src_ref=steer_out.at[pl.ds(pl.multiple_of(other * OWN_BEAMS, OWN_BEAMS), OWN_BEAMS), :],
                dst_ref=steer_in.at[feed],
                send_sem=s_send.at[d],
                recv_sem=s_recv.at[d],
                device_id=(chan, other),
                device_id_type=MESH,
            )
        )
        steer_copies[-1].start()
    own_steer = pltpu.make_async_copy(
        steer_out.at[pl.ds(pl.multiple_of(feed * OWN_BEAMS, OWN_BEAMS), OWN_BEAMS), :],
        steer_in.at[feed],
        s_send.at[0],
    )
    own_steer.start()

    loaded(1)
    convolve(34, 34)
    turn(0)
    mine0 = send_chan(0)
    loaded(2)
    convolve(67, 33)
    loaded(3)
    convolve(100, 31)
    step_one(0, 0, mine0)
    turn(1)
    mine1 = send_chan(1)
    for n in range(1, SUBS):
        step_one(0, n, mine0)

    for n in range(SUBS):
        step_two(0, n)
        step_one(1, n, mine1)

    sums = jnp.sum(power_acc[...], axis=1)
    first = jnp.sum(jnp.where(low8, sums, 0.0), axis=1, keepdims=True)
    second = jnp.sum(jnp.where(low8, 0.0, sums), axis=1, keepdims=True)
    column = jnp.concatenate([first, second], axis=0)
    lane16 = lax.broadcasted_iota(jnp.int32, (OWN, 128), 1)
    sub16 = lax.broadcasted_iota(jnp.int32, (OWN, 128), 0)
    power_row[...] = jnp.sum(
        jnp.where(lax.rem(lane16, OWN) == sub16, column, 0.0), axis=0, keepdims=True
    )
    p_own = pltpu.make_async_copy(power_row, powers.at[feed, chan], own_sem.at[2])
    p_own.start()
    p_copies = []
    for d in range(1, CHAN_DEVS):
        copy = pltpu.make_async_remote_copy(
            src_ref=power_row,
            dst_ref=powers.at[feed, chan],
            send_sem=p_send.at[d],
            recv_sem=p_recv.at[d],
            device_id=(lax.rem(chan + d, CHAN_DEVS), feed),
            device_id_type=MESH,
        )
        copy.start()
        p_copies.append(copy)

    for copy in steer_copies:
        copy.wait()
    own_steer.wait()
    for g in range(FEED_DEVS):
        cols = pl.ds(g * FEED_INPUTS, FEED_INPUTS)
        index = steer_in[g].astype(jnp.float32)
        quarter = jnp.floor((index + 32.0) * (1.0 / 64.0))
        angle = (index - 64.0 * quarter) * (2.0 * np.pi / PHASES)
        sq = angle * angle
        cos = 1.0 + sq * (-1.0 / 2 + sq * (1.0 / 24 + sq * (-1.0 / 720 + sq * (1.0 / 40320))))
        sin = angle * (
            1.0 + sq * (-1.0 / 6 + sq * (1.0 / 120 + sq * (-1.0 / 5040 + sq * (1.0 / 362880))))
        )
        swap = (quarter == 1.0) | (quarter == 3.0)
        cos_neg = (quarter == 1.0) | (quarter == 2.0)
        sin_neg = (quarter == 2.0) | (quarter == 3.0)
        cos_mag = jnp.where(swap, sin, cos)
        sin_mag = jnp.where(swap, cos, sin)
        weight_buf[0:OWN_BEAMS, cols] = jnp.where(cos_neg, -cos_mag, cos_mag).astype(jnp.bfloat16)
        weight_buf[OWN_BEAMS : 2 * OWN_BEAMS, cols] = jnp.where(sin_neg, -sin_mag, sin_mag).astype(
            jnp.bfloat16
        )

    weight_copy = pltpu.make_async_copy(weight_buf, weights, out_sem)
    weight_copy.start()

    for n in range(SUBS):
        step_two(1, n)

    p_own.wait()
    for copy in p_copies:
        copy.wait()
    q_copies = []
    for d in range(1, FEED_DEVS):
        copy = pltpu.make_async_remote_copy(
            src_ref=powers.at[feed],
            dst_ref=powers.at[feed],
            send_sem=q_send.at[d],
            recv_sem=q_recv.at[d],
            device_id=(chan, lax.rem(feed + d, FEED_DEVS)),
            device_id_type=MESH,
        )
        copy.start()
        q_copies.append(copy)

    for h in range(2):
        for n in range(SUBS):
            step_three(h, n)

    for copy in a_copies:
        copy.wait_send()
    for copy in q_copies:
        copy.wait()
    weight_copy.wait()
    for h in range(2):
        for n in range(SUBS):
            for kind in ("other fore", "pass fore", "other back"):
                landed(h, n, kind)
    for copy in made.values():
        copy.wait_send()


def correlate_kernel(
    spectra, powers, flags, flag_row, weights, vis, beam,
    product, col_scale, row_scale, out_sem,
):
    feed = lax.axis_index("feed")
    lane = lax.broadcasted_iota(jnp.int32, (CHAN_DEVS, 128), 1)
    power = jnp.zeros((CHAN_DEVS, 128), jnp.float32)
    for f in range(FEED_DEVS):
        power = jnp.where(lane // OWN == f, powers[f].reshape(CHAN_DEVS, 128), power)
    scale = lax.rsqrt(power / (BAND * NT) + EPSILON)
    col_scale[...] = scale * flags[...].astype(jnp.float32)
    for n in range(2):
        one = col_scale[pl.ds(2 * feed + n, 1), :] * (1.0 / NT)
        row_scale[128 * n : 128 * (n + 1), :] = jnp.broadcast_to(one, (128, 128)).T

    def parts(c, first, count):
        return jnp.concatenate(
            [
                spectra[h, pl.ds(first, count), :, pl.ds(c * OWN, OWN), :].reshape(count * 128, 128)
                for h in range(2)
            ],
            axis=1,
        )

    def swapped(c, h):
        own = spectra[h, pl.ds(2 * feed, 2), :, pl.ds(c * OWN, OWN), :]
        own = own.reshape(256, 128).astype(jnp.float32)
        lane = lax.broadcasted_iota(jnp.int32, (256, 128), 1)
        turned = pltpu.roll(own, HALF_T, 1)
        return jnp.where(lane < HALF_T, turned, -turned).astype(jnp.bfloat16)

    def stores(c):
        copies = []
        step = FEED_INPUTS // OUT_PARTS
        for p in range(2):
            for n in range(OUT_PARTS):
                rows = pl.ds(n * step, step)
                copies.append(
                    pltpu.make_async_copy(
                        product.at[p, c, rows, :], vis.at[p, c, rows, :], out_sem.at[c]
                    )
                )
        return copies

    @pl.loop(0, PER_CHAN)
    def _(c):

        own = parts(c, 2 * feed, 2)
        turned = jnp.concatenate([swapped(c, 0), swapped(c, 1)], axis=1)
        left = jnp.concatenate([own, turned], axis=0)
        rows = row_scale[...]
        for n in range(INPUTS // 256):
            both = lax.dot_general(
                left,
                parts(c, 2 * n, 2),
                (((1,), (1,)), ((), ())),
                preferred_element_type=jnp.float32,
            )
            for m in range(2):
                scale = rows * col_scale[2 * n + m : 2 * n + m + 1, :]
                out = pl.ds((2 * n + m) * 128, 128)
                product[0, c, :, out] = both[0:256, 128 * m : 128 * (m + 1)] * scale
                product[1, c, :, out] = both[256:512, 128 * m : 128 * (m + 1)] * scale
        for copy in stores(c):
            copy.start()

    good = weights[...] * flag_row[...].astype(jnp.float32).astype(jnp.bfloat16)
    lane = lax.broadcasted_iota(jnp.int32, (OWN_BEAMS, 128), 1)
    for c in range(PER_CHAN):
        sums = jnp.dot(
            good, parts(c, 0, CHAN_DEVS), preferred_element_type=jnp.float32
        )
        halves = []
        for h in range(2):
            cols = slice(128 * h, 128 * (h + 1))
            cos_part = sums[0:OWN_BEAMS, cols]
            sin_part = pltpu.roll(sums[OWN_BEAMS : 2 * OWN_BEAMS, cols], HALF_T, 1)
            field = cos_part + jnp.where(lane < HALF_T, -sin_part, sin_part)
            square = field * field
            halves.append(square + pltpu.roll(square, HALF_T, 1))
        beam[:, c, :] = jnp.where(lane < HALF_T, halves[0], halves[1]) * (1.0 / INPUTS)
    for c in range(PER_CHAN):
        whole = product.at[:, c]
        pltpu.make_async_copy(whole, whole, out_sem.at[c]).wait()


def channelize_turn(table, raw_volts, channel_gains, steer_index):
    hbm = pl.BlockSpec(memory_space=pl.ANY)
    bf16, f32 = jnp.bfloat16, jnp.float32
    dma = pltpu.SemaphoreType.DMA
    spectra, powers, weights = pl.pallas_call(
        turn_kernel,
        name="channelize_turn",
        out_shape=(
            jax.ShapeDtypeStruct((2, CHAN_DEVS, FEED_DEVS, UNIT, 128), bf16),
            jax.ShapeDtypeStruct((FEED_DEVS, CHAN_DEVS, 1, 128), f32),
            jax.ShapeDtypeStruct((2 * OWN_BEAMS, INPUTS), bf16),
        ),
        in_specs=[hbm] * 4,
        out_specs=(hbm, hbm, hbm),
        scratch_shapes=[
            pltpu.VMEM((SLABS * OWN, BLOCK), bf16),
            pltpu.VMEM((BLOCK, TAPS * 128), bf16),
            pltpu.VMEM((SLABS * OWN, TAPS * 128), f32),
            pltpu.VMEM((HALF_T * OWN, 128), f32),
            pltpu.VMEM((BAND * OWN, 128), f32),
            pltpu.VMEM((2, BAND * OWN, 128), bf16),
            pltpu.VMEM((2, OWN, BAND), f32),
            pltpu.VMEM((BEAMS, FEED_INPUTS), jnp.int32),
            pltpu.VMEM((8, 8, 128), f32),
            pltpu.VMEM((1, 128), f32),
            pltpu.VMEM((BEAMS, FEED_INPUTS), bf16),
            pltpu.VMEM((FEED_DEVS, OWN_BEAMS, FEED_INPUTS), bf16),
            pltpu.VMEM((2 * OWN_BEAMS, INPUTS), bf16),
            dma((4,)),
            dma,
            dma((3,)),
            dma((3,)),
            dma((2, 2 * CHAN_DEVS)),
            dma((2, 2, SUBS)),
            dma((2, KINDS, SUBS)),
            dma((2, KINDS, SUBS)),
            dma((FEED_DEVS,)),
            dma((FEED_DEVS,)),
            dma((CHAN_DEVS,)),
            dma((CHAN_DEVS,)),
            dma((FEED_DEVS,)),
            dma((FEED_DEVS,)),
            dma,
        ],
        compiler_params=pltpu.CompilerParams(
            collective_id=0, has_side_effects=True, vmem_limit_bytes=46000 * 1024
        ),
        cost_estimate=pl.CostEstimate(
            flops=2 * SLABS * OWN * BLOCK * 512, bytes_accessed=20_000_000, transcendentals=0
        ),
    )(raw_volts, table, jnp.transpose(channel_gains, (0, 2, 1)), steer_index)
    return spectra, powers, weights


def correlate(spectra, powers, feed_flags, weights):
    f32 = jnp.float32
    hbm = pl.BlockSpec(memory_space=pl.ANY)
    vmem = pl.BlockSpec(memory_space=pltpu.VMEM)
    dma = pltpu.SemaphoreType.DMA
    return pl.pallas_call(
        correlate_kernel,
        name="correlate",
        out_shape=(
            jax.ShapeDtypeStruct((2, PER_CHAN, FEED_INPUTS, INPUTS), f32),
            jax.ShapeDtypeStruct((OWN_BEAMS, PER_CHAN, NT), f32),
        ),
        in_specs=[vmem] * 5,
        out_specs=(hbm, vmem),
        scratch_shapes=[
            pltpu.VMEM((2, PER_CHAN, FEED_INPUTS, INPUTS), f32),
            pltpu.VMEM((CHAN_DEVS, 128), f32),
            pltpu.VMEM((256, 128), f32),
            dma((PER_CHAN,)),
        ],
        compiler_params=pltpu.CompilerParams(vmem_limit_bytes=28 * 2**20),
        cost_estimate=pl.CostEstimate(
            flops=2_700_000_000, bytes_accessed=22_000_000, transcendentals=0
        ),
    )(spectra, powers, feed_flags.reshape(CHAN_DEVS, 128), feed_flags.reshape(1, INPUTS), weights)


def solution(mesh):
    table = np.stack([filter_table()] * 4)
    in_specs = (P(("chan", "feed"), None), P(None, None, ("chan", "feed")), P(), P(None, "feed"))
    out_specs = (P(None, "chan", "feed", None), P("feed", "chan", None))

    def body(raw_volts, channel_gains, feed_flags, steer_index):
        spectra, powers, weights = channelize_turn(
            jnp.asarray(table), raw_volts, channel_gains, steer_index
        )
        return correlate(spectra, powers, feed_flags, weights)

    return jax.shard_map(
        body, mesh=mesh, in_specs=in_specs, out_specs=out_specs, check_vma=False
    )
```

```python
import functools

import jax
import jax.numpy as jnp
import ml_dtypes
import numpy as np
from jax import lax
from jax.experimental import pallas as pl
from jax.experimental.pallas import tpu as pltpu
from jax.sharding import PartitionSpec as P

CHANS = 1024
INPUTS = 2048
TAPS = 4
PHASES = 256
NT = 128
BAND = 64
BEAMS = 512
BLOCK = 2 * CHANS
EPSILON = 1e-06

CHAN_DEVS = 16
FEED_DEVS = 8
OWN = 16
PER_CHAN = BAND // CHAN_DEVS
UNIT = PER_CHAN * OWN
HALF_T = NT // 2
SLABS = NT + TAPS - 1
SUBS = 4
SUB = CHAN_DEVS // SUBS
OWN_BEAMS = BEAMS // FEED_DEVS
FEED_INPUTS = INPUTS // FEED_DEVS
KINDS = 6
OUT_PARTS = 4
MESH = pl.DeviceIdType.MESH


def filter_table():
    full_len = TAPS * BLOCK
    pos = np.arange(full_len, dtype=np.float64)
    centred = (pos + 0.5) / full_len - 0.5
    window = np.sinc(TAPS * centred) * (0.5 - 0.5 * np.cos(2.0 * np.pi * (pos + 0.5) / full_len))
    window = window / np.sqrt(np.sum(window * window))
    channel = CHANS // 2 - BAND // 2 + np.arange(BAND)
    turn = (np.arange(BLOCK)[:, None] * channel[None, :]) % BLOCK
    angle = 2.0 * np.pi / BLOCK * turn
    weights = window.reshape(TAPS, BLOCK)[:, :, None]
    table = np.concatenate([weights * np.cos(angle), -(weights * np.sin(angle))], axis=2)
    return np.transpose(table, (1, 0, 2)).reshape(BLOCK, TAPS * 2 * BAND).astype(ml_dtypes.bfloat16)


def turn_kernel(
    raw, table, gains, steer, spectra, powers, weights,
    volts, tab, conv, summed, turned, outbox, gain_buf, steer_buf, power_acc, power_row,
    steer_out, steer_in, weight_buf,
    load_sem, tab_sem, small_sem, own_sem, a_send, a_recv, b_send, b_recv,
    s_send, s_recv, p_send, p_recv, q_send, q_recv, out_sem,
):
    chan = lax.axis_index("chan")
    feed = lax.axis_index("feed")
    x = feed // 2
    row = feed % 2

    def feed_at(dx, across):
        r = 1 - row if across else row
        return lax.rem(x + dx + 4, 4) * 2 + r

    right = (chan, feed_at(1, False))
    left = (chan, feed_at(-1, False))
    over = (chan, feed_at(0, True))

    barrier = pltpu.get_barrier_semaphore()
    plane = [
        ((half, d), across)
        for half in range(SUBS)
        for across in range(2)
        for d in range(SUB)
        if (half, d, across) != (0, 0, 0)
    ]

    def near(k):
        if SUBS == 2:
            return (chan // SUB + k) % 2
        return (chan // 8 + k // 2) % 2 * 2 + (chan // 4 + k) % 2

    def plane_peer(half, d):
        return near(half) * SUB + lax.rem(chan + d, SUB)

    distant = [(dx, across) for dx in (1, 3, 2) for across in (False, True)]
    for (half, d), across in plane:
        pl.semaphore_signal(
            barrier,
            inc=1,
            device_id=(plane_peer(half, d), feed_at(0, bool(across))),
            device_id_type=MESH,
        )
    for dx, across in distant:
        pl.semaphore_signal(
            barrier, inc=1, device_id=(chan, feed_at(dx, across)), device_id_type=MESH
        )

    tab_copy = pltpu.make_async_copy(table.at[0], tab, tab_sem)
    tab_copy.start()
    gain_copy = pltpu.make_async_copy(gains, gain_buf, small_sem.at[0])
    gain_copy.start()
    steer_copy = pltpu.make_async_copy(steer, steer_buf, small_sem.at[1])
    steer_copy.start()
    groups = [(0, 34), (34, 34), (68, 32), (100, 31)]

    def fetch(g):
        first, count = groups[g]

        @pl.loop(0, count)
        def _(n):
            s = first + n
            pltpu.make_async_copy(
                raw.at[:, pl.ds(pl.multiple_of(s * BLOCK, BLOCK), BLOCK)],
                volts.at[pl.ds(pl.multiple_of(s * OWN, OWN), OWN), :],
                load_sem.at[g],
            ).start()

    fetch(0)
    fetch(1)

    gain_copy.wait()
    pair_re = jnp.concatenate([gain_buf[0, 0:8], gain_buf[0, 8:16]], axis=1)
    pair_im = jnp.concatenate([gain_buf[1, 0:8], gain_buf[1, 8:16]], axis=1)
    lane8 = lax.broadcasted_iota(jnp.int32, (8, 128), 1)
    low8 = lane8 < BAND

    low = lax.broadcasted_iota(jnp.int32, (HALF_T, 128), 1) < BAND

    def loaded(g):
        first, count = groups[g]
        rows = volts.at[pl.ds(first * OWN, count * OWN), :]
        pltpu.make_async_copy(rows, rows, load_sem.at[g]).wait()

    def convolve(first, count):
        conv[pl.ds(first * OWN, count * OWN), :] = jnp.dot(
            volts[pl.ds(first * OWN, count * OWN), :], tab[...], preferred_element_type=jnp.float32
        )

    def turn(h):
        total = None
        for k in range(TAPS):
            part = conv[pl.ds((HALF_T * h + k) * OWN, HALF_T * OWN), 128 * k : 128 * (k + 1)]
            total = part if total is None else total + part
        summed[0 : HALF_T * OWN, :] = total
        for i in range(8):
            a = summed[pl.ds(i, HALF_T, stride=OWN), :]
            b = summed[pl.ds(i + 8, HALF_T, stride=OWN), :]
            re = jnp.where(low, a, pltpu.roll(b, BAND, 1))
            im = jnp.where(low, pltpu.roll(a, BAND, 1), b)
            g_re = pair_re[i : i + 1]
            g_im = pair_im[i : i + 1]
            spec_re = (g_re * re - g_im * im).astype(jnp.bfloat16).astype(jnp.float32)
            spec_im = (g_re * im + g_im * re).astype(jnp.bfloat16).astype(jnp.float32)
            power = spec_re * spec_re + spec_im * spec_im
            power = jnp.sum(power.reshape(HALF_T // 8, 8, 128), axis=0)
            if h == 0:
                power_acc[i] = power
            else:
                power_acc[i] = power_acc[i] + power
            flipped = jnp.concatenate([spec_re, spec_im], axis=0).T
            turned[pl.ds(i, BAND, stride=OWN), :] = flipped[0:BAND]
            turned[pl.ds(i + 8, BAND, stride=OWN), :] = flipped[BAND : 2 * BAND]
        outbox[h] = turned[0 : BAND * OWN, :].astype(jnp.bfloat16)

    a_copies = []

    def send_chan(h):
        mine = pltpu.make_async_copy(
            outbox.at[h, pl.ds(pl.multiple_of(chan * UNIT, UNIT), UNIT), :],
            spectra.at[h, chan, feed],
            own_sem.at[h],
        )
        mine.start()
        for n, ((half, d), across) in enumerate(plane):
            other = plane_peer(half, d)
            copy = pltpu.make_async_remote_copy(
                src_ref=outbox.at[h, pl.ds(pl.multiple_of(other * UNIT, UNIT), UNIT), :],
                dst_ref=spectra.at[h, chan, feed],
                send_sem=a_send.at[h, n],
                recv_sem=a_recv.at[h, across, half],
                device_id=(other, feed_at(0, bool(across))),
                device_id_type=MESH,
            )
            copy.start()
            a_copies.append(copy)
        return mine

    def arrived(h, across, half):
        count = SUB - 1 if (across, half) == (0, 0) else SUB
        rows = spectra.at[h, pl.ds(0, count), 0]
        pltpu.make_async_copy(rows, rows, a_recv.at[h, across, half]).wait()

    sub_of = [near(k) for k in range(SUBS)]

    def spread(h, n, kind, origin, target):
        block = spectra.at[h, pl.ds(pl.multiple_of(sub_of[n] * SUB, SUB), SUB), origin]
        return pltpu.make_async_remote_copy(
            src_ref=block,
            dst_ref=block,
            send_sem=b_send.at[h, kind, n],
            recv_sem=b_recv.at[h, kind, n],
            device_id=target,
            device_id_type=MESH,
        )

    plans = []
    for n in range(SUBS):
        fore, back, s = (right, left, 1) if n % 2 == 0 else (left, right, -1)
        plans.append(
            {
                "own fore": (feed, fore),
                "own back": (feed, back),
                "pass fore": (feed_at(-s, False), fore),
                "pass over": (feed_at(s, False), over),
                "other fore": (feed_at(0, True), fore),
                "other back": (feed_at(s, True), back),
            }
        )
    kinds = list(plans[0])
    made = {}

    def start(h, n, kind):
        origin, target = plans[n][kind]
        made[h, n, kind] = spread(h, n, kinds.index(kind), origin, target)
        made[h, n, kind].start()

    def landed(h, n, kind):
        made[h, n, kind].wait_recv()

    def step_one(h, n, mine):
        if n == 0:
            mine.wait()
        arrived(h, 0, n)
        start(h, n, "own back")
        start(h, n, "own fore")
        arrived(h, 1, n)
        start(h, n, "other fore")

    def step_two(h, n):
        landed(h, n, "own back")
        start(h, n, "pass over")
        landed(h, n, "own fore")
        start(h, n, "pass fore")

    def step_three(h, n):
        landed(h, n, "pass over")
        start(h, n, "other back")

    loaded(0)
    tab_copy.wait()
    fetch(2)
    fetch(3)
    convolve(0, 34)

    steer_copy.wait()
    steer_out[...] = steer_buf[...].astype(jnp.float32).astype(jnp.bfloat16)
    pl.semaphore_wait(barrier, len(plane) + len(distant))
    steer_copies = []
    for d in range(1, FEED_DEVS):
        other = lax.rem(feed + d, FEED_DEVS)
        steer_copies.append(
            pltpu.make_async_remote_copy(
                src_ref=steer_out.at[pl.ds(pl.multiple_of(other * OWN_BEAMS, OWN_BEAMS), OWN_BEAMS), :],
                dst_ref=steer_in.at[feed],
                send_sem=s_send.at[d],
                recv_sem=s_recv.at[d],
                device_id=(chan, other),
                device_id_type=MESH,
            )
        )
        steer_copies[-1].start()
    own_steer = pltpu.make_async_copy(
        steer_out.at[pl.ds(pl.multiple_of(feed * OWN_BEAMS, OWN_BEAMS), OWN_BEAMS), :],
        steer_in.at[feed],
        s_send.at[0],
    )
    own_steer.start()

    loaded(1)
    convolve(34, 34)
    turn(0)
    mine0 = send_chan(0)
    loaded(2)
    convolve(67, 33)
    loaded(3)
    convolve(100, 31)
    step_one(0, 0, mine0)
    turn(1)
    mine1 = send_chan(1)
    for n in range(1, SUBS):
        step_one(0, n, mine0)

    for n in range(SUBS):
        step_two(0, n)
        step_one(1, n, mine1)

    sums = jnp.sum(power_acc[...], axis=1)
    first = jnp.sum(jnp.where(low8, sums, 0.0), axis=1, keepdims=True)
    second = jnp.sum(jnp.where(low8, 0.0, sums), axis=1, keepdims=True)
    column = jnp.concatenate([first, second], axis=0)
    lane16 = lax.broadcasted_iota(jnp.int32, (OWN, 128), 1)
    sub16 = lax.broadcasted_iota(jnp.int32, (OWN, 128), 0)
    power_row[...] = jnp.sum(
        jnp.where(lax.rem(lane16, OWN) == sub16, column, 0.0), axis=0, keepdims=True
    )
    p_own = pltpu.make_async_copy(power_row, powers.at[feed, chan], own_sem.at[2])
    p_own.start()
    p_copies = []
    for d in range(1, CHAN_DEVS):
        copy = pltpu.make_async_remote_copy(
            src_ref=power_row,
            dst_ref=powers.at[feed, chan],
            send_sem=p_send.at[d],
            recv_sem=p_recv.at[d],
            device_id=(lax.rem(chan + d, CHAN_DEVS), feed),
            device_id_type=MESH,
        )
        copy.start()
        p_copies.append(copy)

    for copy in steer_copies:
        copy.wait()
    own_steer.wait()
    for g in range(FEED_DEVS):
        cols = pl.ds(g * FEED_INPUTS, FEED_INPUTS)
        index = steer_in[g].astype(jnp.float32)
        quarter = jnp.floor((index + 32.0) * (1.0 / 64.0))
        angle = (index - 64.0 * quarter) * (2.0 * np.pi / PHASES)
        sq = angle * angle
        cos = 1.0 + sq * (-1.0 / 2 + sq * (1.0 / 24 + sq * (-1.0 / 720 + sq * (1.0 / 40320))))
        sin = angle * (
            1.0 + sq * (-1.0 / 6 + sq * (1.0 / 120 + sq * (-1.0 / 5040 + sq * (1.0 / 362880))))
        )
        swap = (quarter == 1.0) | (quarter == 3.0)
        cos_neg = (quarter == 1.0) | (quarter == 2.0)
        sin_neg = (quarter == 2.0) | (quarter == 3.0)
        cos_mag = jnp.where(swap, sin, cos)
        sin_mag = jnp.where(swap, cos, sin)
        weight_buf[0:OWN_BEAMS, cols] = jnp.where(cos_neg, -cos_mag, cos_mag).astype(jnp.bfloat16)
        weight_buf[OWN_BEAMS : 2 * OWN_BEAMS, cols] = jnp.where(sin_neg, -sin_mag, sin_mag).astype(
            jnp.bfloat16
        )

    weight_copy = pltpu.make_async_copy(weight_buf, weights, out_sem)
    weight_copy.start()

    for n in range(SUBS):
        step_two(1, n)

    p_own.wait()
    for copy in p_copies:
        copy.wait()
    q_copies = []
    for d in range(1, FEED_DEVS):
        copy = pltpu.make_async_remote_copy(
            src_ref=powers.at[feed],
            dst_ref=powers.at[feed],
            send_sem=q_send.at[d],
            recv_sem=q_recv.at[d],
            device_id=(chan, lax.rem(feed + d, FEED_DEVS)),
            device_id_type=MESH,
        )
        copy.start()
        q_copies.append(copy)

    for h in range(2):
        for n in range(SUBS):
            step_three(h, n)

    for copy in a_copies:
        copy.wait_send()
    for copy in q_copies:
        copy.wait()
    weight_copy.wait()
    for h in range(2):
        for n in range(SUBS):
            for kind in ("other fore", "pass fore", "other back"):
                landed(h, n, kind)
    for copy in made.values():
        copy.wait_send()


def correlate_kernel(
    spectra, powers, flags, flag_row, weights, vis, beam,
    product, col_scale, row_scale, out_sem,
):
    feed = lax.axis_index("feed")
    lane = lax.broadcasted_iota(jnp.int32, (CHAN_DEVS, 128), 1)
    power = jnp.zeros((CHAN_DEVS, 128), jnp.float32)
    for f in range(FEED_DEVS):
        power = jnp.where(lane // OWN == f, powers[f].reshape(CHAN_DEVS, 128), power)
    scale = lax.rsqrt(power / (BAND * NT) + EPSILON)
    col_scale[...] = scale * flags[...].astype(jnp.float32)
    for n in range(2):
        one = col_scale[pl.ds(2 * feed + n, 1), :] * (1.0 / NT)
        row_scale[128 * n : 128 * (n + 1), :] = jnp.broadcast_to(one, (128, 128)).T

    def parts(c, first, count):
        return jnp.concatenate(
            [
                spectra[h, pl.ds(first, count), :, pl.ds(c * OWN, OWN), :].reshape(count * 128, 128)
                for h in range(2)
            ],
            axis=1,
        )

    def swapped(c, h):
        own = spectra[h, pl.ds(2 * feed, 2), :, pl.ds(c * OWN, OWN), :]
        own = own.reshape(256, 128).astype(jnp.float32)
        lane = lax.broadcasted_iota(jnp.int32, (256, 128), 1)
        turned = pltpu.roll(own, HALF_T, 1)
        return jnp.where(lane < HALF_T, turned, -turned).astype(jnp.bfloat16)

    def stores(c):
        copies = []
        step = FEED_INPUTS // OUT_PARTS
        for p in range(2):
            for n in range(OUT_PARTS):
                rows = pl.ds(n * step, step)
                copies.append(
                    pltpu.make_async_copy(
                        product.at[p, c, rows, :], vis.at[p, c, rows, :], out_sem.at[c]
                    )
                )
        return copies

    @pl.loop(0, PER_CHAN)
    def _(c):

        own = parts(c, 2 * feed, 2)
        turned = jnp.concatenate([swapped(c, 0), swapped(c, 1)], axis=1)
        left = jnp.concatenate([own, turned], axis=0)
        rows = row_scale[...]
        for n in range(INPUTS // 256):
            both = lax.dot_general(
                left,
                parts(c, 2 * n, 2),
                (((1,), (1,)), ((), ())),
                preferred_element_type=jnp.float32,
            )
            for m in range(2):
                scale = rows * col_scale[2 * n + m : 2 * n + m + 1, :]
                out = pl.ds((2 * n + m) * 128, 128)
                product[0, c, :, out] = both[0:256, 128 * m : 128 * (m + 1)] * scale
                product[1, c, :, out] = both[256:512, 128 * m : 128 * (m + 1)] * scale
        for copy in stores(c):
            copy.start()

    good = weights[...] * flag_row[...].astype(jnp.float32).astype(jnp.bfloat16)
    lane = lax.broadcasted_iota(jnp.int32, (OWN_BEAMS, 128), 1)
    for c in range(PER_CHAN):
        sums = jnp.dot(
            good, parts(c, 0, CHAN_DEVS), preferred_element_type=jnp.float32
        )
        halves = []
        for h in range(2):
            cols = slice(128 * h, 128 * (h + 1))
            cos_part = sums[0:OWN_BEAMS, cols]
            sin_part = pltpu.roll(sums[OWN_BEAMS : 2 * OWN_BEAMS, cols], HALF_T, 1)
            field = cos_part + jnp.where(lane < HALF_T, -sin_part, sin_part)
            square = field * field
            halves.append(square + pltpu.roll(square, HALF_T, 1))
        beam[:, c, :] = jnp.where(lane < HALF_T, halves[0], halves[1]) * (1.0 / INPUTS)
    for c in range(PER_CHAN):
        whole = product.at[:, c]
        pltpu.make_async_copy(whole, whole, out_sem.at[c]).wait()


def channelize_turn(table, raw_volts, channel_gains, steer_index):
    hbm = pl.BlockSpec(memory_space=pl.ANY)
    bf16, f32 = jnp.bfloat16, jnp.float32
    dma = pltpu.SemaphoreType.DMA
    spectra, powers, weights = pl.pallas_call(
        turn_kernel,
        name="channelize_turn",
        out_shape=(
            jax.ShapeDtypeStruct((2, CHAN_DEVS, FEED_DEVS, UNIT, 128), bf16),
            jax.ShapeDtypeStruct((FEED_DEVS, CHAN_DEVS, 1, 128), f32),
            jax.ShapeDtypeStruct((2 * OWN_BEAMS, INPUTS), bf16),
        ),
        in_specs=[hbm] * 4,
        out_specs=(hbm, hbm, hbm),
        scratch_shapes=[
            pltpu.VMEM((SLABS * OWN, BLOCK), bf16),
            pltpu.VMEM((BLOCK, TAPS * 128), bf16),
            pltpu.VMEM((SLABS * OWN, TAPS * 128), f32),
            pltpu.VMEM(((HALF_T + 1) * OWN, 128), f32),
            pltpu.VMEM(((BAND + 1) * OWN, 128), f32),
            pltpu.VMEM((2, BAND * OWN, 128), bf16),
            pltpu.VMEM((2, OWN, BAND), f32),
            pltpu.VMEM((BEAMS, FEED_INPUTS), jnp.int32),
            pltpu.VMEM((8, 8, 128), f32),
            pltpu.VMEM((1, 128), f32),
            pltpu.VMEM((BEAMS, FEED_INPUTS), bf16),
            pltpu.VMEM((FEED_DEVS, OWN_BEAMS, FEED_INPUTS), bf16),
            pltpu.VMEM((2 * OWN_BEAMS, INPUTS), bf16),
            dma((4,)),
            dma,
            dma((3,)),
            dma((3,)),
            dma((2, 2 * CHAN_DEVS)),
            dma((2, 2, SUBS)),
            dma((2, KINDS, SUBS)),
            dma((2, KINDS, SUBS)),
            dma((FEED_DEVS,)),
            dma((FEED_DEVS,)),
            dma((CHAN_DEVS,)),
            dma((CHAN_DEVS,)),
            dma((FEED_DEVS,)),
            dma((FEED_DEVS,)),
            dma,
        ],
        compiler_params=pltpu.CompilerParams(
            collective_id=0, has_side_effects=True, vmem_limit_bytes=46000 * 1024
        ),
        cost_estimate=pl.CostEstimate(
            flops=2 * SLABS * OWN * BLOCK * 512, bytes_accessed=20_000_000, transcendentals=0
        ),
    )(raw_volts, table, jnp.transpose(channel_gains, (0, 2, 1)), steer_index)
    return spectra, powers, weights


def correlate(spectra, powers, feed_flags, weights):
    f32 = jnp.float32
    hbm = pl.BlockSpec(memory_space=pl.ANY)
    vmem = pl.BlockSpec(memory_space=pltpu.VMEM)
    dma = pltpu.SemaphoreType.DMA
    return pl.pallas_call(
        correlate_kernel,
        name="correlate",
        out_shape=(
            jax.ShapeDtypeStruct((2, PER_CHAN, FEED_INPUTS, INPUTS), f32),
            jax.ShapeDtypeStruct((OWN_BEAMS, PER_CHAN, NT), f32),
        ),
        in_specs=[vmem] * 5,
        out_specs=(hbm, vmem),
        scratch_shapes=[
            pltpu.VMEM((2, PER_CHAN, FEED_INPUTS, INPUTS), f32),
            pltpu.VMEM((CHAN_DEVS, 128), f32),
            pltpu.VMEM((256, 128), f32),
            dma((PER_CHAN,)),
        ],
        compiler_params=pltpu.CompilerParams(vmem_limit_bytes=28 * 2**20),
        cost_estimate=pl.CostEstimate(
            flops=2_700_000_000, bytes_accessed=22_000_000, transcendentals=0
        ),
    )(spectra, powers, feed_flags.reshape(CHAN_DEVS, 128), feed_flags.reshape(1, INPUTS), weights)


def solution(mesh):
    table = np.stack([filter_table()] * 4)
    in_specs = (P(("chan", "feed"), None), P(None, None, ("chan", "feed")), P(), P(None, "feed"))
    out_specs = (P(None, "chan", "feed", None), P("feed", "chan", None))

    def body(raw_volts, channel_gains, feed_flags, steer_index):
        spectra, powers, weights = channelize_turn(
            jnp.asarray(table), raw_volts, channel_gains, steer_index
        )
        return correlate(spectra, powers, feed_flags, weights)

    return jax.shard_map(
        body, mesh=mesh, in_specs=in_specs, out_specs=out_specs, check_vma=False
    )
```
